256 devices in a mesh: lat: 16 (over y_lo, x, core), lon: 16 (over z, y_hi).
Axes of the slice: x: 4, y: 4 (y_hi: 2, y_lo: 2; y = y_hi * 2 + y_lo), z: 8, core: 2. Of those that a mesh axis runs over, the one named last changes fastest.
Arguments:
- fields: float32 [2, 192, 768, 192], P(None, 'lat', 'lon'), may hold values from -6 to 6
- cotangent: float32 [2, 192, 768, 192], P(None, 'lat', 'lon'), may hold values from -6 to 6
- norm_gain: float32 [192], replicated, may hold values from 0.1 to 1.9
- qkv_weight: float32 [192, 576], replicated, may hold values from -0.4375 to 0.4375
- out_weight: float32 [192, 192], replicated, may hold values from -0.4375 to 0.4375
- bias_table: float32 [32, 6, 3312], P('lat'), may hold values from -310 to 310, as said below
Outputs:
- branch: float32 [2, 192, 768, 192], P(None, 'lat', 'lon')
- grad_fields: float32 [2, 192, 768, 192], P(None, 'lat', 'lon')
- grad_gain: float32 [192], replicated
- grad_qkv: float32 [192, 576], replicated
- grad_out: float32 [192, 192], replicated
- grad_table: float32 [32, 6, 3312], P('lat')
The draws below stay inside these ranges and needn't reach their ends.
Inputs may be any that keep to these rules, and one draw needn't show every extreme that they name: `bias_table`: entries of the bias tables.
All inputs are finite; a program needn't handle non-finite values.
Results may differ from the reference program's by a relative error of at most 0.0003.
Values sent between devices are 32-bit elements; how exact they have to be, the bound alone decides.
A program may use at most 128 MiB of HBM per device.

```python
import math
import jax
import jax.numpy as jnp
from jax import lax

D = 192
HEADS = 6
WIN_LAT = 6
WIN_LON = 12
CODES = 3312
LEVELS = 2
LAT = 192
LON = 768
LATWIN = 32
CELLS = 294912


def draw_bias_table(key, part):
    key = jax.random.fold_in(key, 11)
    keys = jax.random.split(key, 1)
    shape = (LATWIN, HEADS, CODES)
    return jax.random.normal(keys[0], shape, jnp.float32)


def steps_of(stream_key, shape, pieces, least, high):
    gain, own = 1.0, jax.random.fold_in(stream_key, 6)
    for position, blocks in pieces:
        steps = jnp.exp(jax.random.uniform(jax.random.fold_in(own, position), (blocks,), jnp.float32, least / len(pieces), high / len(pieces)))
        gain = gain * jnp.repeat(steps, shape[position] // blocks).reshape([-1 if axis == position else 1 for axis in range(len(shape))])
    return gain


def scatter_about(stream_key, dims, deviation, bound, pieces=(), dtype=jnp.bfloat16):
    drawn = jax.random.normal(stream_key, dims, jnp.float32) * deviation
    if len(pieces) > 0:
        drawn = steps_of(stream_key, dims, pieces, -0.22, 0.18) * drawn
    return jnp.clip(drawn, min=-bound, max=bound).astype(dtype)


def setup_inputs(seed: int = 0) -> dict:
    key_list = jax.random.split(jax.random.key(seed), 7)
    return {
        "fields": scatter_about(key_list[0], (LEVELS, LAT, LON, D), 1.0, 6.0, ((1, 16), (2, 16)), jnp.float32),
        "cotangent": scatter_about(key_list[1], (LEVELS, LAT, LON, D), 1.0, 6.0, ((1, 16), (2, 16)), jnp.float32),
        "norm_gain": jnp.clip(1.0 + 0.18 * jax.random.normal(key_list[2], (D,), jnp.float32), 0.1, 1.9),
        "qkv_weight": scatter_about(key_list[3], (D, 3 * D), D ** -0.5, 0.4375, (), jnp.float32),
        "out_weight": scatter_about(key_list[4], (D, D), D ** -0.5, 0.4375, (), jnp.float32),
        "bias_table": draw_bias_table(jax.random.fold_in(key_list[6], 71), 0),
    }


EPSILON = 1e-05
MASKED = -1000000000.0
HIGHEST = lax.Precision.HIGHEST

def offset_table(columns):
    diffs = (jnp.arange(columns)[None, :] - jnp.arange(columns)[:, None] + columns - 1).reshape(-1)
    return (jnp.arange(2 * columns - 1)[:, None] == diffs[None, :]).astype(jnp.float32)

def window_row(field_row, grad_row, table_row, on_seam, norm_gain, qkv_weight, out_weight, head_count):
    levels, lat_window, columns, channels = field_row.shape
    lon_window = WIN_LON
    blocks_lon = columns // lon_window
    tokens = levels * lat_window * lon_window
    outer_count = levels * lat_window
    head_size = channels // head_count
    spread = offset_table(lon_window)

    def to_windows(array):
        shaped = array.reshape(levels, lat_window, blocks_lon, lon_window, channels)
        return shaped.transpose(2, 0, 1, 3, 4).reshape(blocks_lon, tokens, channels)

    def from_windows(array):
        shaped = array.reshape(blocks_lon, levels, lat_window, lon_window, channels)
        return shaped.transpose(1, 2, 0, 3, 4).reshape(levels, lat_window, columns, channels)
    inputs = to_windows(field_row)
    upstream = to_windows(grad_row)
    centre = lax.optimization_barrier(jnp.mean(inputs, axis=-1, keepdims=True))
    centred = inputs - centre
    inverse_std = lax.rsqrt(lax.optimization_barrier(jnp.mean(centred * centred, axis=-1, keepdims=True)) + EPSILON)
    normed = centred * inverse_std
    scaled = normed * norm_gain
    projected = jnp.einsum('wtd,de->wte', scaled, qkv_weight, precision=HIGHEST)
    projected = projected.reshape(blocks_lon, tokens, 3, head_count, head_size)
    queries = projected[:, :, 0]
    key_rows = projected[:, :, 1]
    values = projected[:, :, 2]
    factor = head_size ** (-0.5)
    table_blocks = table_row.reshape(head_count * outer_count * outer_count, 2 * lon_window - 1)
    bias_full = jnp.dot(table_blocks, spread, precision=HIGHEST, preferred_element_type=jnp.float32)
    bias_full = bias_full.reshape(head_count, outer_count, outer_count, lon_window, lon_window)
    bias_full = bias_full.transpose(0, 1, 3, 2, 4).reshape(head_count, tokens, tokens)
    lat_position = jnp.arange(tokens) // lon_window % lat_window
    upper_half = lat_position < lat_window // 2
    masked = jnp.logical_and(on_seam, upper_half[:, None] != upper_half[None, :])
    scores = jnp.einsum('wqhe,wkhe->whqk', queries, key_rows, precision=HIGHEST) * factor + bias_full[None]
    scores = jnp.where(masked[None, None], MASKED, scores)
    largest = lax.optimization_barrier(jnp.max(scores, axis=-1, keepdims=True))
    exponent = jnp.exp(scores - largest)
    attention = exponent / lax.optimization_barrier(jnp.sum(exponent, axis=-1, keepdims=True))
    mixed = jnp.einsum('whqk,wkhe->wqhe', attention, values, precision=HIGHEST).reshape(blocks_lon, tokens, channels)
    output = jnp.einsum('wtd,de->wte', mixed, out_weight, precision=HIGHEST)
    grad_out = jnp.einsum('wtd,wte->de', mixed, upstream, precision=HIGHEST)
    grad_mixed = jnp.einsum('wte,de->wtd', upstream, out_weight, precision=HIGHEST)
    grad_mixed = grad_mixed.reshape(blocks_lon, tokens, head_count, head_size)
    grad_attention = jnp.einsum('wqhe,wkhe->whqk', grad_mixed, values, precision=HIGHEST)
    grad_values = jnp.einsum('whqk,wqhe->wkhe', attention, grad_mixed, precision=HIGHEST)
    grad_scores = attention * (grad_attention - lax.optimization_barrier(jnp.sum(grad_attention * attention, axis=-1, keepdims=True)))
    grad_queries = jnp.einsum('whqk,wkhe->wqhe', grad_scores, key_rows, precision=HIGHEST) * factor
    grad_keys = jnp.einsum('whqk,wqhe->wkhe', grad_scores, queries, precision=HIGHEST) * factor
    grad_bias = lax.optimization_barrier(jnp.sum(grad_scores, axis=0)).reshape(head_count, outer_count, lon_window, outer_count, lon_window)
    grad_bias = grad_bias.transpose(0, 1, 3, 2, 4).reshape(head_count * outer_count * outer_count, lon_window * lon_window)
    grad_table = jnp.dot(grad_bias, spread.T, precision=HIGHEST, preferred_element_type=jnp.float32)
    grad_table = grad_table.reshape(head_count, -1)
    grad_projected = jnp.stack([grad_queries, grad_keys, grad_values], axis=2).reshape(blocks_lon, tokens, 3 * channels)
    grad_qkv = jnp.einsum('wtd,wte->de', scaled, grad_projected, precision=HIGHEST)
    grad_scaled = jnp.einsum('wte,de->wtd', grad_projected, qkv_weight, precision=HIGHEST)
    grad_gain = lax.optimization_barrier(jnp.sum(grad_scaled * normed, axis=(0, 1)))
    grad_normed = grad_scaled * norm_gain
    grad_inputs = inverse_std * (grad_normed - lax.optimization_barrier(jnp.mean(grad_normed, axis=-1, keepdims=True)) - normed * lax.optimization_barrier(jnp.mean(grad_normed * normed, axis=-1, keepdims=True)))
    return (from_windows(output), from_windows(grad_inputs), grad_table, grad_qkv, grad_out, grad_gain)

def sweep_rows(fields_win, grads_win, tables, first_row, total_rows, norm_gain, qkv_weight, out_weight, head_count):
    row_count = tables.shape[0]
    lat_window = WIN_LAT
    channels = fields_win.shape[-1]

    def advance(row_index, carried):
        branch_all, inputs_all, table_all, sum_qkv, sum_out, sum_gain = carried
        row_index = row_index.astype(jnp.int32)
        start = row_index * lat_window
        field_row = lax.dynamic_slice_in_dim(fields_win, start, lat_window, 1)
        grad_row = lax.dynamic_slice_in_dim(grads_win, start, lat_window, 1)
        table_row = lax.dynamic_index_in_dim(tables, row_index, 0, keepdims=False)
        on_seam = first_row + row_index == total_rows - 1
        results = window_row(field_row, grad_row, table_row, on_seam, norm_gain, qkv_weight, out_weight, head_count)
        branch_all = lax.dynamic_update_slice_in_dim(branch_all, results[0], start, 1)
        inputs_all = lax.dynamic_update_slice_in_dim(inputs_all, results[1], start, 1)
        table_all = lax.dynamic_update_slice_in_dim(table_all, results[2][None], row_index, 0)
        return (branch_all, inputs_all, table_all, sum_qkv + results[3], sum_out + results[4], sum_gain + results[5])
    initial = (jnp.zeros_like(fields_win), jnp.zeros_like(fields_win), jnp.zeros_like(tables), jnp.zeros((channels, 3 * channels), jnp.float32), jnp.zeros((channels, channels), jnp.float32), jnp.zeros((channels,), jnp.float32))
    return lax.fori_loop(0, row_count, advance, initial)

def reference(fields, cotangent, norm_gain, qkv_weight, out_weight, bias_table):
    half_lat = WIN_LAT // 2
    half_lon = WIN_LON // 2
    fields_win = jnp.roll(fields, (-half_lat, -half_lon), axis=(1, 2))
    grads_win = jnp.roll(cotangent, (-half_lat, -half_lon), axis=(1, 2))
    results = sweep_rows(fields_win, grads_win, bias_table, 0, LATWIN, norm_gain, qkv_weight, out_weight, HEADS)
    factor = 1.0 / math.sqrt(CELLS)
    branch = jnp.roll(results[0], (half_lat, half_lon), axis=(1, 2))
    grad_fields = jnp.roll(results[1], (half_lat, half_lon), axis=(1, 2))
    return (branch, grad_fields, results[5] * factor, results[3] * factor, results[4] * factor, results[2])
```

```python
import math
import jax
import jax.numpy as jnp
from jax import lax
from jax.experimental import pallas as pl
from jax.experimental.pallas import tpu as pltpu
from jax.sharding import PartitionSpec as P

WIN_LAT = 6
WIN_LON = 12
EPSILON = 1e-05
MASKED = -1000000000.0
HEADS = 6
HEAD = 32
D = 192
TOK = 144
WINDOWS = 8
OUTER = 12
SPAN = 23
F32 = jnp.float32
BF16 = jnp.bfloat16
NN = (((1,), (0,)), ((), ()))
NT = (((1,), (1,)), ((), ()))


def mm(a, b, dims=NN):
    return lax.dot_general(a, b, dims, preferred_element_type=F32)


def split(x):
    hi = x.astype(BF16)
    return hi, (x - hi.astype(F32)).astype(BF16)


def mm3(a, b, dims=NN):
    return mm(a[0], b[0], dims) + mm(a[0], b[1], dims) + mm(a[1], b[0], dims)


def selector(lo, length):
    row = lax.broadcasted_iota(jnp.int32, (length, TOK), 0)
    col = lax.broadcasted_iota(jnp.int32, (length, TOK), 1)
    picked = (col // WIN_LON) * SPAN + col % WIN_LON - lo + WIN_LON - 1
    return (row == picked).astype(F32).astype(BF16)


def compute_kernel(
    seam_ref, ext_f, ext_g, gain_ref, wqkv_ref, wout_ref, table_ref,
    out_b, out_g, chunks_ref, gtable_ref,
    xs, ups, inv_s, n_hi, n_lo, s_hi, s_lo,
    kcat, vcat, q_hi, q_lo, do_hi, do_lo,
    qt, kt, vt, dot_, bias, dsacc, bias_raw,
    mix, dq, dk, dv, mix_t, sums_ref,
):
    factor = HEAD ** (-0.5)
    gain = gain_ref[...]
    w = wqkv_ref[...]
    wq = w[:, :D] * factor
    wk = w[:, D:2 * D]
    wv = w[:, 2 * D:]

    def replicated(m):
        parts = []
        for h in range(HEADS):
            parts += [m[:, h * HEAD:(h + 1) * HEAD]] * 4
        return jnp.concatenate(parts, axis=1)

    wkr = split(replicated(wk))
    wvr = split(replicated(wv))
    wqs = split(wq)
    wt = split(jnp.concatenate([wq.T, wk.T, wv.T], axis=0))
    wo = split(wout_ref[...])
    wks = split(wk)
    wvs = split(wv)
    wqp = split(w[:, :D])

    t0 = table_ref[...]
    t_hi = t0.astype(BF16)
    rest = t0 - t_hi.astype(F32)
    t_mid = rest.astype(BF16)
    t_lo = (rest - t_mid.astype(F32)).astype(BF16)
    for lo in range(WIN_LON):
        sel = selector(lo, OUTER * SPAN)
        part = mm(t_hi, sel) + mm(t_mid, sel) + mm(t_lo, sel)
        bias_raw[:, lo, :] = part
    row = lax.broadcasted_iota(jnp.int32, (TOK, TOK), 0)
    col = lax.broadcasted_iota(jnp.int32, (TOK, TOK), 1)
    half_r = (row // WIN_LON) % WIN_LAT < WIN_LAT // 2
    half_c = (col // WIN_LON) % WIN_LAT < WIN_LAT // 2
    apart = half_r != half_c
    for a in range(2):
        on_seam = seam_ref[0] + a == 31
        cut = jnp.logical_and(apart, on_seam)
        for h in range(HEADS):
            g = a * HEADS + h
            b = bias_raw[g * OUTER:(g + 1) * OUTER].reshape(TOK, TOK)
            bias[g] = jnp.where(cut, MASKED, b.T)
            dsacc[g] = jnp.zeros((TOK, TOK), F32)

    for wi in range(WINDOWS):
        a, b = divmod(wi, 4)
        for l in range(2):
            for r in range(WIN_LAT):
                at = wi * TOK + (l * WIN_LAT + r) * WIN_LON
                c0 = 6 + WIN_LON * b
                xs[at:at + WIN_LON, :] = ext_f[l, a * WIN_LAT + r, c0:c0 + WIN_LON, :]
                ups[at:at + WIN_LON, :] = ext_g[l, a * WIN_LAT + r, c0:c0 + WIN_LON, :]

    @pl.loop(0, WINDOWS)
    def _(wi):
        rows = pl.ds(pl.multiple_of(wi * TOK, TOK), TOK)
        x = xs[rows, :]
        c = x - jnp.mean(x, axis=-1, keepdims=True)
        inv = lax.rsqrt(jnp.mean(c * c, axis=-1, keepdims=True) + EPSILON)
        n = c * inv
        xs[rows, :] = n
        inv_s[rows, :] = jnp.broadcast_to(inv, (TOK, 128))
        nh, nl = split(n)
        n_hi[rows, :] = nh
        n_lo[rows, :] = nl
        s = split(n * gain)
        s_hi[rows, :] = s[0]
        s_lo[rows, :] = s[1]
        pt = mm3(wt, s, NT)
        for i, ref in enumerate((qt, kt, vt)):
            ph, pll = split(pt[i * D:(i + 1) * D])
            for h in range(HEADS):
                a_, b_ = ph[h * HEAD:(h + 1) * HEAD], pll[h * HEAD:(h + 1) * HEAD]
                if ref is qt:
                    ref[wi, h] = jnp.concatenate([a_, b_, a_, b_], axis=0)
                else:
                    ref[wi, h] = jnp.concatenate([a_, b_], axis=0)
        u = split(ups[rows, :])
        dt = split(mm3(wo, u, NT))
        for h in range(HEADS):
            a_, b_ = dt[0][h * HEAD:(h + 1) * HEAD], dt[1][h * HEAD:(h + 1) * HEAD]
            dot_[wi, h] = jnp.concatenate([a_, b_, a_, b_], axis=0)

    lane = lax.broadcasted_iota(jnp.int32, (TOK, 256), 1) % 128
    first = lane < 64

    for j in range(3):
        cols = slice(j * 256, (j + 1) * 256)
        for wr, ref in ((wkr, kcat), (wvr, vcat)):
            wj = (wr[0][:, cols], wr[1][:, cols])

            @pl.loop(0, 2)
            def _(half):
                rows = pl.ds(pl.multiple_of(half * 576, 576), 576)
                p = mm3((s_hi[rows, :], s_lo[rows, :]), wj)
                ph, pll = split(p)
                first_ = lax.broadcasted_iota(jnp.int32, (576, 256), 1) % 128 < 64
                ref[rows, cols] = jnp.where(first_, ph, pll)

    @pl.loop(0, 2)
    def _(half):
        rows = pl.ds(pl.multiple_of(half * 576, 576), 576)
        qh, ql = split(mm3((s_hi[rows, :], s_lo[rows, :]), wqs))
        q_hi[rows, :] = qh
        q_lo[rows, :] = ql
        dh, dl = split(mm3(split(ups[rows, :]), wo, NT))
        do_hi[rows, :] = dh
        do_lo[rows, :] = dl

    head_of = lax.broadcasted_iota(jnp.int32, (TOK, D), 1) // HEAD

    @pl.loop(0, WINDOWS)
    def _(wi):
        rows = pl.ds(pl.multiple_of(wi * TOK, TOK), TOK)
        base = (wi // 4) * HEADS
        dv_acc = jnp.zeros((TOK, D), F32)
        dk_acc = jnp.zeros((TOK, D), F32)
        zero = jnp.zeros((TOK, D), BF16)
        for h in range(HEADS):
            blk = slice(h * 128, (h + 1) * 128)
            st = mm(kcat[rows, blk], qt[wi, h]) + bias[base + h]
            e = jnp.exp(st - jnp.max(st, axis=0, keepdims=True))
            p = e * (1.0 / jnp.sum(e, axis=0, keepdims=True))
            p_hi, p_lo = split(p)
            dp = mm(vcat[rows, blk], dot_[wi, h])
            ds = p * (dp - jnp.sum(p * dp, axis=0, keepdims=True))
            dsacc[base + h] += ds
            ds_hi, ds_lo = split(ds)
            v2 = vt[wi, h]
            m2 = mm(v2, p_hi)
            m = m2[:HEAD] + m2[HEAD:] + mm(v2[:HEAD], p_lo)
            mix_t[h * HEAD:(h + 1) * HEAD, :] = m
            k2 = kt[wi, h]
            g2 = mm(k2, ds_hi)
            g = g2[:HEAD] + g2[HEAD:] + mm(k2[:HEAD], ds_lo)
            dq[wi, h * HEAD:(h + 1) * HEAD, :] = g * factor
            mine = head_of == h
            o_hi = jnp.where(mine, do_hi[rows, :], zero)
            o_lo = jnp.where(mine, do_lo[rows, :], zero)
            dv_acc += mm(p_hi, o_hi) + mm(p_hi, o_lo) + mm(p_lo, o_hi)
            c_hi = jnp.where(mine, q_hi[rows, :], zero)
            c_lo = jnp.where(mine, q_lo[rows, :], zero)
            dk_acc += mm(ds_hi, c_hi) + mm(ds_hi, c_lo) + mm(ds_lo, c_hi)
        dv[rows, :] = dv_acc
        dk[rows, :] = dk_acc
        mix[wi] = mix_t[...]

    sums_ref[...] = jnp.zeros_like(sums_ref)

    @pl.loop(0, WINDOWS)
    def _(wi):
        rows = pl.ds(pl.multiple_of(wi * TOK, TOK), TOK)
        mt = mix[wi]
        mts = split(mt)
        us = split(ups[rows, :])
        sums_ref[:, 3 * D:] += mm3(mts, us)
        q_t = dq[wi]
        n = xs[rows, :]
        nt = split(n.T)
        g_q = split(q_t.T)
        g_k = split(dk[rows, :])
        g_v = split(dv[rows, :])
        sums_ref[:, :D] += mm3(nt, g_q)
        sums_ref[:, D:2 * D] += mm3(nt, g_k)
        sums_ref[:, 2 * D:3 * D] += mm3(nt, g_v)
        grad_scaled = mm3(g_q, wqp, NT) + mm3(g_k, wks, NT) + mm3(g_v, wvs, NT)
        g = grad_scaled * gain
        gi = inv_s[rows, :][:, :1] * (
            g - jnp.mean(g, axis=-1, keepdims=True)
            - n * jnp.mean(g * n, axis=-1, keepdims=True)
        )
        o = mm3(split(mt.T), wo)
        dk[rows, :] = gi
        dv[rows, :] = o

    for wi in range(WINDOWS):
        a, b = divmod(wi, 4)
        for l in range(2):
            for r in range(WIN_LAT):
                at = wi * TOK + (l * WIN_LAT + r) * WIN_LON
                c0 = 6 + WIN_LON * b
                out_b[l, a * WIN_LAT + r, c0:c0 + WIN_LON, :] = dv[at:at + WIN_LON, :]
                out_g[l, a * WIN_LAT + r, c0:c0 + WIN_LON, :] = dk[at:at + WIN_LON, :]

    for g in range(2 * HEADS):
        bias_raw[g * OUTER:(g + 1) * OUTER] = dsacc[g].T.reshape(OUTER, WIN_LON, TOK)
    acc = jnp.zeros((TOK, 384), F32)
    for lo in range(WIN_LON):
        sel = selector(lo, 384)
        d_hi, d_lo = split(bias_raw[:, lo, :])
        acc += mm(d_hi, sel, NT) + mm(d_lo, sel, NT)
    gtable_ref[13:16] = jnp.zeros((3, 32, 128), F32)
    for i in range(18):
        for j in range(3):
            q, s = divmod(i * 3 + j, 4)
            gtable_ref[q, s * 8:s * 8 + 8, :] = acc[i * 8:i * 8 + 8, j * 128:(j + 1) * 128]
    for i in range(24):
        for j in range(6):
            q, s = divmod(i * 6 + j, 9)
            chunks_ref[q, s * 8:s * 8 + 8, :] = sums_ref[i * 8:i * 8 + 8, j * 128:(j + 1) * 128]


def compute(first_row, ext_f, ext_g, gain, wqkv, wout, table):
    vm = pl.BlockSpec(memory_space=pltpu.VMEM)
    rows = WINDOWS * TOK
    scratch = [
        pltpu.VMEM((rows, D), F32), pltpu.VMEM((rows, D), F32), pltpu.VMEM((rows, 128), F32),
        pltpu.VMEM((rows, D), BF16), pltpu.VMEM((rows, D), BF16),
        pltpu.VMEM((rows, D), BF16), pltpu.VMEM((rows, D), BF16),
        pltpu.VMEM((rows, 768), BF16), pltpu.VMEM((rows, 768), BF16),
        pltpu.VMEM((rows, D), BF16), pltpu.VMEM((rows, D), BF16),
        pltpu.VMEM((rows, D), BF16), pltpu.VMEM((rows, D), BF16),
        pltpu.VMEM((WINDOWS, HEADS, 128, TOK), BF16),
        pltpu.VMEM((WINDOWS, HEADS, 64, TOK), BF16),
        pltpu.VMEM((WINDOWS, HEADS, 64, TOK), BF16),
        pltpu.VMEM((WINDOWS, HEADS, 128, TOK), BF16),
        pltpu.VMEM((2 * HEADS, TOK, TOK), F32),
        pltpu.VMEM((2 * HEADS, TOK, TOK), F32),
        pltpu.VMEM((TOK, WIN_LON, TOK), F32),
        pltpu.VMEM((WINDOWS, D, TOK), F32), pltpu.VMEM((WINDOWS, D, TOK), F32),
        pltpu.VMEM((rows, D), F32), pltpu.VMEM((rows, D), F32),
        pltpu.VMEM((D, TOK), F32),
        pltpu.VMEM((D, 4 * D), F32),
    ]
    return pl.pallas_call(
        compute_kernel,
        out_shape=[
            jax.ShapeDtypeStruct((2, 12, 56, D), F32),
            jax.ShapeDtypeStruct((2, 12, 56, D), F32),
            jax.ShapeDtypeStruct((16, 72, 128), F32),
            jax.ShapeDtypeStruct((16, 32, 128), F32),
        ],
        in_specs=[pl.BlockSpec(memory_space=pltpu.SMEM)] + [vm] * 6,
        out_specs=[vm] * 4,
        scratch_shapes=scratch,
        compiler_params=pltpu.CompilerParams(vmem_limit_bytes=60 * 1024 * 1024),
    )(first_row, ext_f, ext_g, gain, wqkv, wout, table)


MESH = pl.DeviceIdType.MESH
LATS = 16
LONS = 16


def halo_in_kernel(f_ref, g_ref, ext_f, ext_g, local_sem, send_sem, recv_sem):
    lat = lax.axis_index("lat")
    lon = lax.axis_index("lon")
    up, down = lax.rem(lat + 1, LATS), lax.rem(lat + LATS - 1, LATS)
    right, left = lax.rem(lon + 1, LONS), lax.rem(lon + LONS - 1, LONS)
    barrier = pltpu.get_barrier_semaphore()
    for target in ((up, lon), (lat, right), (up, right)):
        pl.semaphore_signal(barrier, inc=1, device_id=target, device_id_type=MESH)
    local = []
    for i, (src, dst) in enumerate(((f_ref, ext_f), (g_ref, ext_g))):
        copy = pltpu.make_async_copy(
            src.at[:, pl.ds(3, 9)], dst.at[:, pl.ds(0, 9), pl.ds(0, 48)], local_sem.at[i])
        copy.start()
        local.append(copy)
    pl.semaphore_wait(barrier, 3)
    sent = []
    for i, (src, dst) in enumerate(((f_ref, ext_f), (g_ref, ext_g))):
        pieces = (
            (src.at[:, pl.ds(0, 3)], dst.at[:, pl.ds(9, 3), pl.ds(0, 48)], (down, lon)),
            (src.at[:, pl.ds(3, 9), pl.ds(0, 8)], dst.at[:, pl.ds(0, 9), pl.ds(48, 8)], (lat, left)),
            (src.at[:, pl.ds(0, 3), pl.ds(0, 8)], dst.at[:, pl.ds(9, 3), pl.ds(48, 8)], (down, left)),
        )
        for j, (a, b, target) in enumerate(pieces):
            copy = pltpu.make_async_remote_copy(
                src_ref=a, dst_ref=b, send_sem=send_sem.at[i * 3 + j], recv_sem=recv_sem.at[i * 3 + j],
                device_id=target, device_id_type=MESH)
            copy.start()
            sent.append(copy)
    for copy in local + sent:
        copy.wait()


def halo_in(fields, cotangent):
    anywhere = pl.BlockSpec(memory_space=pl.ANY)
    shape = jax.ShapeDtypeStruct((2, 12, 56, D), F32)
    return pl.pallas_call(
        halo_in_kernel,
        out_shape=[shape, shape],
        in_specs=[anywhere] * 2,
        out_specs=[anywhere] * 2,
        scratch_shapes=[
            pltpu.SemaphoreType.DMA((2,)), pltpu.SemaphoreType.DMA((6,)), pltpu.SemaphoreType.DMA((6,)),
        ],
        compiler_params=pltpu.CompilerParams(collective_id=0, has_side_effects=True),
    )(fields, cotangent)


def reduce_kernel(
    ext_b, ext_g, chunks, tables,
    rows_b, rows_g, cols_b, cols_g, total, table_total,
    recv_a, recv_t, recv_b, part,
    halo_send, halo_recv, a_send, a_recv, t_send, t_recv, b_send, b_recv,
    c_send, c_recv, d_send, d_recv, e_send, e_recv,
):
    lat = lax.axis_index("lat")
    lon = lax.axis_index("lon")
    up, down = lax.rem(lat + 1, LATS), lax.rem(lat + LATS - 1, LATS)
    right, left = lax.rem(lon + 1, LONS), lax.rem(lon + LONS - 1, LONS)
    barrier = pltpu.get_barrier_semaphore()

    @pl.loop(1, LATS)
    def _(k):
        pl.semaphore_signal(barrier, inc=1, device_id=(lax.rem(lat + k, LATS), lon), device_id_type=MESH)
        pl.semaphore_signal(barrier, inc=1, device_id=(lat, lax.rem(lon + k, LONS)), device_id_type=MESH)

    pl.semaphore_signal(barrier, inc=1, device_id=(down, left), device_id_type=MESH)
    pl.semaphore_wait(barrier, 31)

    def remote(src, dst, send, recv, target):
        return pltpu.make_async_remote_copy(
            src_ref=src, dst_ref=dst, send_sem=send, recv_sem=recv, device_id=target, device_id_type=MESH)

    def stage_a(k):
        peer = lax.rem(lat + k, LATS)
        return remote(chunks.at[peer], recv_a.at[k - 1], a_send.at[k - 1], a_recv.at[k - 1], (peer, lon))

    def stage_t(k):
        peer = lax.rem(lon + k, LONS)
        return remote(tables.at[peer], recv_t.at[k - 1], t_send.at[k - 1], t_recv.at[k - 1], (lat, peer))

    @pl.loop(1, LATS)
    def _(k):
        stage_a(k).start()
        stage_t(k).start()

    halos = []
    for i, (src, rows, cols) in enumerate(((ext_b, rows_b, cols_b), (ext_g, rows_g, cols_g))):
        pieces = (
            (src.at[:, pl.ds(9, 3), pl.ds(0, 48)], rows, (up, lon)),
            (src.at[:, pl.ds(0, 9), pl.ds(48, 8)], cols.at[:, pl.ds(3, 9)], (lat, right)),
            (src.at[:, pl.ds(9, 3), pl.ds(48, 8)], cols.at[:, pl.ds(0, 3)], (up, right)),
        )
        for j, (a, b, target) in enumerate(pieces):
            copy = remote(a, b, halo_send.at[i * 3 + j], halo_recv.at[i * 3 + j], target)
            copy.start()
            halos.append(copy)

    @pl.loop(1, LATS)
    def _(k):
        stage_a(k).wait()

    own = chunks[lat]
    for k in range(LATS - 1):
        own += recv_a[k]
    part[...] = own

    def stage_b(k):
        peer = lax.rem(lon + k, LONS)
        at = pl.ds(pl.multiple_of(jnp.minimum(peer, 8) * 8, 8), 8)
        return peer, remote(part.at[at], recv_b.at[k - 1], b_send.at[k - 1], b_recv.at[k - 1], (lat, peer))

    @pl.loop(1, LONS)
    def _(k):
        peer, copy = stage_b(k)

        @pl.when(peer < 9)
        def _():
            copy.start()

    @pl.loop(1, LONS)
    def _(k):
        stage_t(k).wait()

    own = tables[lon]
    for k in range(LONS - 1):
        own += recv_t[k]
    table_total[lon] = own

    def stage_e(k):
        peer = lax.rem(lon + k, LONS)
        return remote(table_total.at[lon], table_total.at[lon], e_send.at[k - 1], e_recv.at[k - 1], (lat, peer))

    def stage_e_in(k):
        peer = lax.rem(lon + LONS - k, LONS)
        return remote(table_total.at[peer], table_total.at[peer], e_send.at[k - 1], e_recv.at[k - 1], (lat, peer))

    @pl.loop(1, LONS)
    def _(k):
        stage_e(k).start()

    mine = pl.ds(pl.multiple_of(jnp.minimum(lon, 8) * 8, 8), 8)

    def stage_c(k):
        peer = lax.rem(lon + k, LONS)
        return remote(total.at[lat, mine], total.at[lat, mine], c_send.at[k - 1], c_recv.at[k - 1], (lat, peer))

    @pl.when(lon < 9)
    def _():
        @pl.loop(1, LONS)
        def _(k):
            stage_b(k)[1].wait_recv()

        tile = part[mine]
        for k in range(LONS - 1):
            tile += recv_b[k]
        total[lat, mine] = tile

        @pl.loop(1, LONS)
        def _(k):
            stage_c(k).start()

    @pl.loop(1, LONS)
    def _(k):
        peer, copy = stage_b(k)

        @pl.when(peer < 9)
        def _():
            copy.wait_send()

    @pl.loop(1, LONS)
    def _(k):
        peer = lax.rem(lon + LONS - k, LONS)
        at = pl.ds(pl.multiple_of(jnp.minimum(peer, 8) * 8, 8), 8)

        @pl.when(peer < 9)
        def _():
            remote(total.at[lat, at], total.at[lat, at], c_send.at[k - 1], c_recv.at[k - 1], (lat, peer)).wait_recv()

    def stage_d(k):
        peer = lax.rem(lat + k, LATS)
        return remote(total.at[lat], total.at[lat], d_send.at[k - 1], d_recv.at[k - 1], (peer, lon))

    @pl.loop(1, LATS)
    def _(k):
        stage_d(k).start()

    @pl.when(lon < 9)
    def _():
        @pl.loop(1, LONS)
        def _(k):
            stage_c(k).wait_send()

    for copy in halos:
        copy.wait()

    @pl.loop(1, LONS)
    def _(k):
        stage_e(k).wait_send()
        stage_e_in(k).wait_recv()

    @pl.loop(1, LATS)
    def _(k):
        stage_d(k).wait_send()
        peer = lax.rem(lat + LATS - k, LATS)
        remote(total.at[peer], total.at[peer], d_send.at[k - 1], d_recv.at[k - 1], (peer, lon)).wait_recv()


def reduce_all(ext_b, ext_g, chunks, tables):
    anywhere = pl.BlockSpec(memory_space=pl.ANY)
    vm = pl.BlockSpec(memory_space=pltpu.VMEM)
    rows = jax.ShapeDtypeStruct((2, 3, 48, D), F32)
    cols = jax.ShapeDtypeStruct((2, 12, 8, D), F32)
    sems = [pltpu.SemaphoreType.DMA((6,))] * 2 + [pltpu.SemaphoreType.DMA((15,))] * 12
    return pl.pallas_call(
        reduce_kernel,
        out_shape=[
            rows, rows, cols, cols,
            jax.ShapeDtypeStruct((16, 72, 128), F32), jax.ShapeDtypeStruct((16, 32, 128), F32),
        ],
        in_specs=[anywhere, anywhere, vm, vm],
        out_specs=[anywhere] * 4 + [vm, vm],
        scratch_shapes=[
            pltpu.VMEM((15, 72, 128), F32), pltpu.VMEM((15, 32, 128), F32),
            pltpu.VMEM((15, 8, 128), F32), pltpu.VMEM((72, 128), F32),
        ] + sems,
        compiler_params=pltpu.CompilerParams(
            collective_id=1, has_side_effects=True, vmem_limit_bytes=32 * 1024 * 1024),
    )(ext_b, ext_g, chunks, tables)


def finish_kernel(
    ext_b, ext_g, rows_b, rows_g, cols_b, cols_g, total, table_total, wqkv_ref, gain_ref,
    branch, grads, gain_out, qkv_out, out_out, table_out, full,
):
    for ext, rows, cols, out in ((ext_b, rows_b, cols_b, branch), (ext_g, rows_g, cols_g, grads)):
        out[:, 0:3] = rows[...]
        out[:, 3:12] = ext[:, 0:9, 0:48, :]
        there = lax.broadcasted_iota(jnp.int32, (2, 12, 8, D), 2) < 6
        out[:, :, 0:8, :] = jnp.where(there, cols[...], out[:, :, 0:8, :])
    scale = 1.0 / math.sqrt(LATS * LONS * WINDOWS * TOK)
    for i in range(24):
        for j in range(6):
            q, s = divmod(i * 6 + j, 9)
            full[i * 8:i * 8 + 8, j * 128:(j + 1) * 128] = total[q, s * 8:s * 8 + 8, :] * scale
    raw = full[:, :3 * D]
    gain_out[...] = jnp.sum(raw * wqkv_ref[...], axis=1, keepdims=True)
    qkv_out[...] = raw * gain_ref[...]
    out_out[...] = full[:, 3 * D:]
    for i in range(18):
        for j in range(3):
            q, s = divmod(i * 3 + j, 4)
            wide = min(128, OUTER * SPAN - j * 128)
            table_out[i * 8:i * 8 + 8, j * 128:j * 128 + wide] = table_total[q, s * 8:s * 8 + 8, :wide]


def finish(ext_b, ext_g, rows_b, rows_g, cols_b, cols_g, total, table_total, wqkv, gain):
    vm = pl.BlockSpec(memory_space=pltpu.VMEM)
    whole = jax.ShapeDtypeStruct((2, 12, 48, D), F32)
    return pl.pallas_call(
        finish_kernel,
        out_shape=[
            whole, whole, jax.ShapeDtypeStruct((D, 1), F32), jax.ShapeDtypeStruct((D, 3 * D), F32),
            jax.ShapeDtypeStruct((D, D), F32), jax.ShapeDtypeStruct((TOK, OUTER * SPAN), F32),
        ],
        in_specs=[vm] * 10,
        out_specs=[vm] * 6,
        scratch_shapes=[pltpu.VMEM((D, 4 * D), F32)],
        compiler_params=pltpu.CompilerParams(vmem_limit_bytes=32 * 1024 * 1024),
    )(ext_b, ext_g, rows_b, rows_g, cols_b, cols_g, total, table_total, wqkv, gain)


def on_device(fields, cotangent, norm_gain, qkv_weight, out_weight, bias_table):
    ext_f, ext_g = halo_in(fields, cotangent)
    first_row = (lax.axis_index("lat") * 2).astype(jnp.int32).reshape(1)
    table = bias_table.reshape(TOK, OUTER * SPAN)
    win_b, win_g, chunks, tables = compute(
        first_row, ext_f, ext_g, norm_gain.reshape(1, D), qkv_weight, out_weight, table)
    rows_b, rows_g, cols_b, cols_g, total, table_total = reduce_all(win_b, win_g, chunks, tables)
    branch, grad_fields, gain, qkv, out, gtable = finish(
        win_b, win_g, rows_b, rows_g, cols_b, cols_g, total, table_total, qkv_weight, norm_gain.reshape(D, 1))
    return branch, grad_fields, gain.reshape(D), qkv, out, gtable.reshape(bias_table.shape)


def solution(mesh):
    cells = P(None, "lat", "lon", None)
    rows = P("lat", None, None)
    return jax.shard_map(
        on_device,
        mesh=mesh,
        in_specs=(cells, cells, P(), P(), P(), rows),
        out_specs=(cells, cells, P(), P(), P(), rows),
        check_vma=False,
    )
```

```python
import math
import jax
import jax.numpy as jnp
from jax import lax
from jax.experimental import pallas as pl
from jax.experimental.pallas import tpu as pltpu
from jax.sharding import PartitionSpec as P

WIN_LAT = 6
WIN_LON = 12
EPSILON = 1e-05
MASKED = -1000000000.0
HEADS = 6
HEAD = 32
D = 192
TOK = 144
WINDOWS = 8
OUTER = 12
SPAN = 23
F32 = jnp.float32
BF16 = jnp.bfloat16
NN = (((1,), (0,)), ((), ()))
NT = (((1,), (1,)), ((), ()))


def mm(a, b, dims=NN):
    return lax.dot_general(a, b, dims, preferred_element_type=F32)


def split(x):
    hi = x.astype(BF16)
    return hi, (x - hi.astype(F32)).astype(BF16)


def mm3(a, b, dims=NN):
    return mm(a[0], b[0], dims) + mm(a[0], b[1], dims) + mm(a[1], b[0], dims)


def selector(lo, length):
    row = lax.broadcasted_iota(jnp.int32, (length, TOK), 0)
    col = lax.broadcasted_iota(jnp.int32, (length, TOK), 1)
    picked = (col // WIN_LON) * SPAN + col % WIN_LON - lo + WIN_LON - 1
    return (row == picked).astype(F32).astype(BF16)


MESH = pl.DeviceIdType.MESH
LATS = 16
LONS = 16
CHIPS = 8


def remote(src, dst, send, recv, target):
    return pltpu.make_async_remote_copy(
        src_ref=src, dst_ref=dst, send_sem=send, recv_sem=recv, device_id=target, device_id_type=MESH)


def every(first, last):
    return pl.loop(first, last, unroll=True)


def main_kernel(
    f_ref, g_ref, gain_ref, wqkv_ref, wout_ref, table_ref,
    out_b, out_g, rows_b, rows_g, cols_b, cols_g, total, table_total,
    ext_f, ext_g,
    xs, ups, inv_s, n_hi, n_lo, s_hi, s_lo,
    kcat, vcat, q_hi, q_lo, do_hi, do_lo,
    qt, kt, vt, dot_, bias, dsacc, bias_raw,
    mix, dq, dk, dv, mix_t, sums_ref, chunks, tables,
    half, recv_p, recv_a, recv_t, recv_b, part,
    local_sem, in_send, in_recv, halo_send, halo_recv, p_send, p_recv, a_send, a_recv,
    t_send, t_recv, b_send, b_recv, c_send, c_recv, d_send, d_recv, m_send, m_recv, e_send, e_recv,
):
    lat = lax.axis_index("lat")
    lon = lax.axis_index("lon")
    chip = lax.div(lat, 2)
    core = lax.rem(lat, 2)
    mate = chip * 2 + 1 - core
    up, down = lax.rem(lat + 1, LATS), lax.rem(lat + LATS - 1, LATS)
    right, left = lax.rem(lon + 1, LONS), lax.rem(lon + LONS - 1, LONS)
    local = []
    for i, (src, dst) in enumerate(((f_ref, ext_f), (g_ref, ext_g))):
        copy = pltpu.make_async_copy(
            src.at[:, pl.ds(3, 9)], dst.at[:, pl.ds(0, 9), pl.ds(0, 48)], local_sem.at[i])
        copy.start()
        local.append(copy)
    barrier = pltpu.get_barrier_semaphore()

    def greet(target):
        pl.semaphore_signal(barrier, inc=1, device_id=target, device_id_type=MESH)

    @every(1, LONS)
    def _(k):
        greet((lat, lax.rem(lon + k, LONS)))

    @every(1, LATS)
    def _(k):
        greet((lax.rem(lat + k, LATS), lon))

    greet((up, right))
    greet((down, left))
    pl.semaphore_wait(barrier, 32)
    halos_in = []
    for i, (src, dst) in enumerate(((f_ref, ext_f), (g_ref, ext_g))):
        pieces = (
            (src.at[:, pl.ds(3, 9), pl.ds(0, 8)], dst.at[:, pl.ds(0, 9), pl.ds(48, 8)], (lat, left)),
            (src.at[:, pl.ds(0, 3), pl.ds(0, 8)], dst.at[:, pl.ds(9, 3), pl.ds(48, 8)], (down, left)),
            (src.at[:, pl.ds(0, 3)], dst.at[:, pl.ds(9, 3), pl.ds(0, 48)], (down, lon)),
        )
        for j, (a, b, target) in enumerate(pieces):
            copy = remote(a, b, in_send.at[i * 3 + j], in_recv.at[i * 3 + j], target)
            copy.start()
            halos_in.append(copy)

    factor = HEAD ** (-0.5)
    gain = gain_ref[...]
    w = wqkv_ref[...]
    wq = w[:, :D] * factor
    wk = w[:, D:2 * D]
    wv = w[:, 2 * D:]

    def replicated(m):
        parts = []
        for h in range(HEADS):
            parts += [m[:, h * HEAD:(h + 1) * HEAD]] * 4
        return jnp.concatenate(parts, axis=1)

    wkr = split(replicated(wk))
    wvr = split(replicated(wv))
    wqs = split(wq)
    wt = split(jnp.concatenate([wq.T, wk.T, wv.T], axis=0))
    wo = split(wout_ref[...])
    wks = split(wk)
    wvs = split(wv)
    wqp = split(w[:, :D])

    t0 = table_ref[...]
    t_hi = t0.astype(BF16)
    rest = t0 - t_hi.astype(F32)
    t_mid = rest.astype(BF16)
    t_lo = (rest - t_mid.astype(F32)).astype(BF16)
    for lo in range(WIN_LON):
        sel = selector(lo, OUTER * SPAN)
        bias_raw[:, lo, :] = mm(t_hi, sel) + mm(t_mid, sel) + mm(t_lo, sel)
    row = lax.broadcasted_iota(jnp.int32, (TOK, TOK), 0)
    col = lax.broadcasted_iota(jnp.int32, (TOK, TOK), 1)
    half_r = (row // WIN_LON) % WIN_LAT < WIN_LAT // 2
    half_c = (col // WIN_LON) % WIN_LAT < WIN_LAT // 2
    apart = half_r != half_c
    for a in range(2):
        on_seam = lat * 2 + a == 31
        cut = jnp.logical_and(apart, on_seam)
        for h in range(HEADS):
            g = a * HEADS + h
            b = bias_raw[g * OUTER:(g + 1) * OUTER].reshape(TOK, TOK)
            bias[g] = jnp.where(cut, MASKED, b.T)
            dsacc[g] = jnp.zeros((TOK, TOK), F32)

    for copy in local + halos_in:
        copy.wait()

    for wi in range(WINDOWS):
        a, b = divmod(wi, 4)
        for l in range(2):
            for r in range(WIN_LAT):
                at = wi * TOK + (l * WIN_LAT + r) * WIN_LON
                c0 = 6 + WIN_LON * b
                xs[at:at + WIN_LON, :] = ext_f[l, a * WIN_LAT + r, c0:c0 + WIN_LON, :]
                ups[at:at + WIN_LON, :] = ext_g[l, a * WIN_LAT + r, c0:c0 + WIN_LON, :]

    @pl.loop(0, WINDOWS)
    def _(wi):
        rows = pl.ds(pl.multiple_of(wi * TOK, TOK), TOK)
        x = xs[rows, :]
        c = x - jnp.mean(x, axis=-1, keepdims=True)
        inv = lax.rsqrt(jnp.mean(c * c, axis=-1, keepdims=True) + EPSILON)
        n = c * inv
        xs[rows, :] = n
        inv_s[rows, :] = jnp.broadcast_to(inv, (TOK, 128))
        nh, nl = split(n)
        n_hi[rows, :] = nh
        n_lo[rows, :] = nl
        s = split(n * gain)
        s_hi[rows, :] = s[0]
        s_lo[rows, :] = s[1]
        pt = mm3(wt, s, NT)
        for i, ref in enumerate((qt, kt, vt)):
            ph, pll = split(pt[i * D:(i + 1) * D])
            for h in range(HEADS):
                a_, b_ = ph[h * HEAD:(h + 1) * HEAD], pll[h * HEAD:(h + 1) * HEAD]
                if ref is qt:
                    ref[wi, h] = jnp.concatenate([a_, b_, a_, b_], axis=0)
                else:
                    ref[wi, h] = jnp.concatenate([a_, b_], axis=0)
        u = split(ups[rows, :])
        dt = split(mm3(wo, u, NT))
        for h in range(HEADS):
            a_, b_ = dt[0][h * HEAD:(h + 1) * HEAD], dt[1][h * HEAD:(h + 1) * HEAD]
            dot_[wi, h] = jnp.concatenate([a_, b_, a_, b_], axis=0)

    lane = lax.broadcasted_iota(jnp.int32, (TOK, 256), 1) % 128
    first = lane < 64

    for j in range(3):
        cols = slice(j * 256, (j + 1) * 256)
        for wr, ref in ((wkr, kcat), (wvr, vcat)):
            wj = (wr[0][:, cols], wr[1][:, cols])

            @pl.loop(0, 2)
            def _(half):
                rows = pl.ds(pl.multiple_of(half * 576, 576), 576)
                p = mm3((s_hi[rows, :], s_lo[rows, :]), wj)
                ph, pll = split(p)
                first_ = lax.broadcasted_iota(jnp.int32, (576, 256), 1) % 128 < 64
                ref[rows, cols] = jnp.where(first_, ph, pll)

    @pl.loop(0, 2)
    def _(half):
        rows = pl.ds(pl.multiple_of(half * 576, 576), 576)
        qh, ql = split(mm3((s_hi[rows, :], s_lo[rows, :]), wqs))
        q_hi[rows, :] = qh
        q_lo[rows, :] = ql
        dh, dl = split(mm3(split(ups[rows, :]), wo, NT))
        do_hi[rows, :] = dh
        do_lo[rows, :] = dl

    head_of = lax.broadcasted_iota(jnp.int32, (TOK, D), 1) // HEAD

    @pl.loop(0, WINDOWS)
    def _(wi):
        rows = pl.ds(pl.multiple_of(wi * TOK, TOK), TOK)
        base = (wi // 4) * HEADS
        dv_acc = jnp.zeros((TOK, D), F32)
        dk_acc = jnp.zeros((TOK, D), F32)
        zero = jnp.zeros((TOK, D), BF16)
        for h in range(HEADS):
            blk = slice(h * 128, (h + 1) * 128)
            st = mm(kcat[rows, blk], qt[wi, h]) + bias[base + h]
            e = jnp.exp(st - jnp.max(st, axis=0, keepdims=True))
            p = e * (1.0 / jnp.sum(e, axis=0, keepdims=True))
            p_hi, p_lo = split(p)
            dp = mm(vcat[rows, blk], dot_[wi, h])
            ds = p * (dp - jnp.sum(p * dp, axis=0, keepdims=True))
            dsacc[base + h] += ds
            ds_hi, ds_lo = split(ds)
            v2 = vt[wi, h]
            m2 = mm(v2, p_hi)
            m = m2[:HEAD] + m2[HEAD:] + mm(v2[:HEAD], p_lo)
            mix_t[h * HEAD:(h + 1) * HEAD, :] = m
            k2 = kt[wi, h]
            g2 = mm(k2, ds_hi)
            g = g2[:HEAD] + g2[HEAD:] + mm(k2[:HEAD], ds_lo)
            dq[wi, h * HEAD:(h + 1) * HEAD, :] = g * factor
            mine = head_of == h
            o_hi = jnp.where(mine, do_hi[rows, :], zero)
            o_lo = jnp.where(mine, do_lo[rows, :], zero)
            dv_acc += mm(p_hi, o_hi) + mm(p_hi, o_lo) + mm(p_lo, o_hi)
            c_hi = jnp.where(mine, q_hi[rows, :], zero)
            c_lo = jnp.where(mine, q_lo[rows, :], zero)
            dk_acc += mm(ds_hi, c_hi) + mm(ds_hi, c_lo) + mm(ds_lo, c_hi)
        dv[rows, :] = dv_acc
        dk[rows, :] = dk_acc
        mix[wi] = mix_t[...]

    sums_ref[...] = jnp.zeros_like(sums_ref)

    @pl.loop(0, WINDOWS)
    def _(wi):
        rows = pl.ds(pl.multiple_of(wi * TOK, TOK), TOK)
        nt = split(xs[rows, :].T)
        sums_ref[:, 3 * D:] += mm3(split(mix[wi]), split(ups[rows, :]))
        sums_ref[:, :D] += mm3(nt, split(dq[wi].T))
        sums_ref[:, D:2 * D] += mm3(nt, split(dk[rows, :]))
        sums_ref[:, 2 * D:3 * D] += mm3(nt, split(dv[rows, :]))

    for i in range(24):
        for j in range(6):
            q, s = divmod(i * 6 + j, 9)
            chunks[q // 2, q % 2, s * 8:s * 8 + 8, :] = sums_ref[i * 8:i * 8 + 8, j * 128:(j + 1) * 128]
    pair = remote(chunks.at[:, 1 - core], recv_p, p_send, p_recv, (mate, lon))
    pair.start()

    for g in range(2 * HEADS):
        bias_raw[g * OUTER:(g + 1) * OUTER] = dsacc[g].T.reshape(OUTER, WIN_LON, TOK)
    acc = jnp.zeros((TOK, 384), F32)
    for lo in range(WIN_LON):
        sel = selector(lo, 384)
        d_hi, d_lo = split(bias_raw[:, lo, :])
        acc += mm(d_hi, sel, NT) + mm(d_lo, sel, NT)
    tables[13:16] = jnp.zeros((3, 32, 128), F32)
    for i in range(18):
        for j in range(3):
            q, s = divmod(i * 3 + j, 4)
            tables[q, s * 8:s * 8 + 8, :] = acc[i * 8:i * 8 + 8, j * 128:(j + 1) * 128]

    pair.wait()
    half[...] = chunks[:, core] + recv_p[...]

    def stage_a(k):
        peer = lax.rem(chip + k, CHIPS)
        return remote(half.at[peer], recv_a.at[k - 1], a_send.at[k - 1], a_recv.at[k - 1], (peer * 2 + core, lon))

    @every(1, CHIPS)
    def _(k):
        stage_a(k).start()

    def stage_t(k):
        peer = lax.rem(lon + k, LONS)
        return remote(tables.at[peer], recv_t.at[k - 1], t_send.at[k - 1], t_recv.at[k - 1], (lat, peer))

    @every(1, LONS)
    def _(k):
        stage_t(k).start()

    def rest_of(wi):
        rows = pl.ds(pl.multiple_of(wi * TOK, TOK), TOK)
        n = xs[rows, :]
        grad_scaled = (
            mm3(split(dq[wi].T), wqp, NT) + mm3(split(dk[rows, :]), wks, NT) + mm3(split(dv[rows, :]), wvs, NT)
        )
        g = grad_scaled * gain
        gi = inv_s[rows, :][:, :1] * (
            g - jnp.mean(g, axis=-1, keepdims=True)
            - n * jnp.mean(g * n, axis=-1, keepdims=True)
        )
        o = mm3(split(mix[wi].T), wo)
        dk[rows, :] = gi
        dv[rows, :] = o

    def scatter(wi):
        a, b = divmod(wi, 4)
        for l in range(2):
            for r in range(WIN_LAT):
                at = wi * TOK + (l * WIN_LAT + r) * WIN_LON
                c0 = 6 + WIN_LON * b
                out_b[l, a * WIN_LAT + r, c0:c0 + WIN_LON, :] = dv[at:at + WIN_LON, :]
                out_g[l, a * WIN_LAT + r, c0:c0 + WIN_LON, :] = dk[at:at + WIN_LON, :]

    @pl.loop(3, WINDOWS)
    def _(wi):
        rest_of(wi)

    for wi in range(3, WINDOWS):
        scatter(wi)

    halos = []
    for i, (src, rows, cols) in enumerate(((out_b, rows_b, cols_b), (out_g, rows_g, cols_g))):
        pieces = (
            (src.at[:, pl.ds(0, 9), pl.ds(48, 8)], cols.at[:, pl.ds(3, 9)], (lat, right)),
            (src.at[:, pl.ds(9, 3), pl.ds(48, 8)], cols.at[:, pl.ds(0, 3)], (up, right)),
            (src.at[:, pl.ds(9, 3), pl.ds(0, 48)], rows, (up, lon)),
        )
        for j, (a, b, target) in enumerate(pieces):
            copy = remote(a, b, halo_send.at[i * 3 + j], halo_recv.at[i * 3 + j], target)
            copy.start()
            halos.append(copy)

    @every(1, CHIPS)
    def _(k):
        stage_a(k).wait()

    own = half[chip]
    for k in range(CHIPS - 1):
        own += recv_a[k]
    part[...] = own

    def stage_b(k):
        peer = lax.rem(lon + k, LONS)
        at = pl.ds(pl.multiple_of(jnp.minimum(peer, 8) * 8, 8), 8)
        return peer, remote(part.at[at], recv_b.at[k - 1], b_send.at[k - 1], b_recv.at[k - 1], (lat, peer))

    @every(1, LONS)
    def _(k):
        peer, copy = stage_b(k)

        @pl.when(peer < 9)
        def _():
            copy.start()

    @pl.loop(0, 3)
    def _(wi):
        rest_of(wi)

    for wi in range(3):
        scatter(wi)

    mine = pl.ds(pl.multiple_of(jnp.minimum(lon, 8) * 8, 8), 8)

    def stage_c(k):
        peer = lax.rem(lon + k, LONS)
        here = total.at[chip, core, mine]
        return remote(here, here, c_send.at[k - 1], c_recv.at[k - 1], (lat, peer))

    @pl.when(lon < 9)
    def _():
        @every(1, LONS)
        def _(k):
            stage_b(k)[1].wait_recv()

        tile = part[mine]
        for k in range(LONS - 1):
            tile += recv_b[k]
        total[chip, core, mine] = tile

        @every(1, LONS)
        def _(k):
            stage_c(k).start()

    @every(1, LONS)
    def _(k):
        stage_t(k).wait()

    own = tables[lon]
    for k in range(LONS - 1):
        own += recv_t[k]
    table_total[lon] = own

    def stage_e(k):
        peer = lax.rem(lon + k, LONS)
        return remote(table_total.at[lon], table_total.at[lon], e_send.at[k - 1], e_recv.at[k - 1], (lat, peer))

    @every(1, LONS)
    def _(k):
        stage_e(k).start()

    @every(1, LONS)
    def _(k):
        peer = lax.rem(lon + LONS - k, LONS)
        at = pl.ds(pl.multiple_of(jnp.minimum(peer, 8) * 8, 8), 8)

        @pl.when(peer < 9)
        def _():
            there = total.at[chip, core, at]
            remote(there, there, c_send.at[k - 1], c_recv.at[k - 1], (lat, peer)).wait_recv()

    def stage_d(k):
        peer = lax.rem(chip + k, CHIPS)
        here = total.at[chip, core]
        return remote(here, here, d_send.at[k - 1], d_recv.at[k - 1], (peer * 2 + core, lon))

    @every(1, CHIPS)
    def _(k):
        stage_d(k).start()

    @every(1, LONS)
    def _(k):
        peer, copy = stage_b(k)

        @pl.when(peer < 9)
        def _():
            copy.wait_send()

    @pl.when(lon < 9)
    def _():
        @every(1, LONS)
        def _(k):
            stage_c(k).wait_send()

    @every(1, CHIPS)
    def _(k):
        peer = lax.rem(chip + CHIPS - k, CHIPS)
        there = total.at[peer, core]
        remote(there, there, d_send.at[k - 1], d_recv.at[k - 1], (peer * 2 + core, lon)).wait_recv()

    ours = total.at[:, core]
    swap = remote(ours, ours, m_send, m_recv, (mate, lon))
    swap.start()

    @every(1, CHIPS)
    def _(k):
        stage_d(k).wait_send()

    for copy in halos:
        copy.wait()

    @every(1, LONS)
    def _(k):
        stage_e(k).wait_send()
        peer = lax.rem(lon + LONS - k, LONS)
        there = table_total.at[peer]
        remote(there, there, e_send.at[k - 1], e_recv.at[k - 1], (lat, peer)).wait_recv()

    swap.wait_send()
    theirs = total.at[:, 1 - core]
    remote(theirs, theirs, m_send, m_recv, (mate, lon)).wait_recv()


def main(fields, cotangent, gain, wqkv, wout, table):
    vm = pl.BlockSpec(memory_space=pltpu.VMEM)
    anywhere = pl.BlockSpec(memory_space=pl.ANY)
    rows = WINDOWS * TOK
    DMA = pltpu.SemaphoreType.DMA
    scratch = [
        pltpu.VMEM((2, 12, 56, D), F32), pltpu.VMEM((2, 12, 56, D), F32),
        pltpu.VMEM((rows, D), F32), pltpu.VMEM((rows, D), F32), pltpu.VMEM((rows, 128), F32),
        pltpu.VMEM((rows, D), BF16), pltpu.VMEM((rows, D), BF16),
        pltpu.VMEM((rows, D), BF16), pltpu.VMEM((rows, D), BF16),
        pltpu.VMEM((rows, 768), BF16), pltpu.VMEM((rows, 768), BF16),
        pltpu.VMEM((rows, D), BF16), pltpu.VMEM((rows, D), BF16),
        pltpu.VMEM((rows, D), BF16), pltpu.VMEM((rows, D), BF16),
        pltpu.VMEM((WINDOWS, HEADS, 128, TOK), BF16),
        pltpu.VMEM((WINDOWS, HEADS, 64, TOK), BF16),
        pltpu.VMEM((WINDOWS, HEADS, 64, TOK), BF16),
        pltpu.VMEM((WINDOWS, HEADS, 128, TOK), BF16),
        pltpu.VMEM((2 * HEADS, TOK, TOK), F32),
        pltpu.VMEM((2 * HEADS, TOK, TOK), F32),
        pltpu.VMEM((TOK, WIN_LON, TOK), F32),
        pltpu.VMEM((WINDOWS, D, TOK), F32), pltpu.VMEM((WINDOWS, D, TOK), F32),
        pltpu.VMEM((rows, D), F32), pltpu.VMEM((rows, D), F32),
        pltpu.VMEM((D, TOK), F32),
        pltpu.VMEM((D, 4 * D), F32),
        pltpu.VMEM((8, 2, 72, 128), F32), pltpu.VMEM((16, 32, 128), F32),
        pltpu.VMEM((8, 72, 128), F32), pltpu.VMEM((8, 72, 128), F32), pltpu.VMEM((7, 72, 128), F32),
        pltpu.VMEM((15, 32, 128), F32), pltpu.VMEM((15, 8, 128), F32), pltpu.VMEM((72, 128), F32),
        DMA((2,)), DMA((6,)), DMA((6,)), DMA((6,)), DMA((6,)), DMA, DMA, DMA((7,)), DMA((7,)),
        DMA((15,)), DMA((15,)), DMA((15,)), DMA((15,)), DMA((15,)), DMA((15,)),
        DMA((7,)), DMA((7,)), DMA, DMA, DMA((15,)), DMA((15,)),
    ]
    whole = jax.ShapeDtypeStruct((2, 12, 56, D), F32)
    edge = jax.ShapeDtypeStruct((2, 3, 48, D), F32)
    side = jax.ShapeDtypeStruct((2, 12, 8, D), F32)
    return pl.pallas_call(
        main_kernel,
        out_shape=[
            whole, whole, edge, edge, side, side,
            jax.ShapeDtypeStruct((8, 2, 72, 128), F32), jax.ShapeDtypeStruct((16, 32, 128), F32),
        ],
        in_specs=[anywhere] * 2 + [vm] * 4,
        out_specs=[vm] * 8,
        scratch_shapes=scratch,
        compiler_params=pltpu.CompilerParams(
            collective_id=0, has_side_effects=True, vmem_limit_bytes=60 * 1024 * 1024),
    )(fields, cotangent, gain, wqkv, wout, table)


def finish_kernel(
    ext_b, ext_g, rows_b, rows_g, cols_b, cols_g, total, table_total, wqkv_ref, gain_ref,
    branch, grads, gain_out, qkv_out, out_out, table_out, full,
):
    for ext, rows, cols, out in ((ext_b, rows_b, cols_b, branch), (ext_g, rows_g, cols_g, grads)):
        out[:, 0:3] = rows[...]
        out[:, 3:12] = ext[:, 0:9, 0:48, :]
        there = lax.broadcasted_iota(jnp.int32, (2, 12, 8, D), 2) < 6
        out[:, :, 0:8, :] = jnp.where(there, cols[...], out[:, :, 0:8, :])
    scale = 1.0 / math.sqrt(LATS * LONS * WINDOWS * TOK)
    for i in range(24):
        for j in range(6):
            q, s = divmod(i * 6 + j, 9)
            full[i * 8:i * 8 + 8, j * 128:(j + 1) * 128] = total[q // 2, q % 2, s * 8:s * 8 + 8, :] * scale
    raw = full[:, :3 * D]
    gain_out[...] = jnp.sum(raw * wqkv_ref[...], axis=1, keepdims=True)
    qkv_out[...] = raw * gain_ref[...]
    out_out[...] = full[:, 3 * D:]
    for i in range(18):
        for j in range(3):
            q, s = divmod(i * 3 + j, 4)
            wide = min(128, OUTER * SPAN - j * 128)
            table_out[i * 8:i * 8 + 8, j * 128:j * 128 + wide] = table_total[q, s * 8:s * 8 + 8, :wide]


def finish(ext_b, ext_g, rows_b, rows_g, cols_b, cols_g, total, table_total, wqkv, gain):
    vm = pl.BlockSpec(memory_space=pltpu.VMEM)
    whole = jax.ShapeDtypeStruct((2, 12, 48, D), F32)
    return pl.pallas_call(
        finish_kernel,
        out_shape=[
            whole, whole, jax.ShapeDtypeStruct((D, 1), F32), jax.ShapeDtypeStruct((D, 3 * D), F32),
            jax.ShapeDtypeStruct((D, D), F32), jax.ShapeDtypeStruct((TOK, OUTER * SPAN), F32),
        ],
        in_specs=[vm] * 10,
        out_specs=[vm] * 6,
        scratch_shapes=[pltpu.VMEM((D, 4 * D), F32)],
        compiler_params=pltpu.CompilerParams(vmem_limit_bytes=60 * 1024 * 1024),
    )(ext_b, ext_g, rows_b, rows_g, cols_b, cols_g, total, table_total, wqkv, gain)


def on_device(fields, cotangent, norm_gain, qkv_weight, out_weight, bias_table):
    table = bias_table.reshape(TOK, OUTER * SPAN)
    win_b, win_g, rows_b, rows_g, cols_b, cols_g, total, table_total = main(
        fields, cotangent, norm_gain.reshape(1, D), qkv_weight, out_weight, table)
    branch, grad_fields, gain, qkv, out, gtable = finish(
        win_b, win_g, rows_b, rows_g, cols_b, cols_g, total, table_total, qkv_weight, norm_gain.reshape(D, 1))
    return branch, grad_fields, gain.reshape(D), qkv, out, gtable.reshape(bias_table.shape)


def solution(mesh):
    cells = P(None, "lat", "lon", None)
    rows = P("lat", None, None)
    return jax.shard_map(
        on_device,
        mesh=mesh,
        in_specs=(cells, cells, P(), P(), P(), rows),
        out_specs=(cells, cells, P(), P(), P(), rows),
        check_vma=False,
    )
```

```python
import math
import jax
import jax.numpy as jnp
from jax import lax
from jax.experimental import pallas as pl
from jax.experimental.pallas import tpu as pltpu
from jax.sharding import PartitionSpec as P

WIN_LAT = 6
WIN_LON = 12
EPSILON = 1e-05
MASKED = -1000000000.0
HEADS = 6
HEAD = 32
D = 192
TOK = 144
WINDOWS = 8
OUTER = 12
SPAN = 23
F32 = jnp.float32
BF16 = jnp.bfloat16
NN = (((1,), (0,)), ((), ()))
NT = (((1,), (1,)), ((), ()))


def mm(a, b, dims=NN):
    return lax.dot_general(a, b, dims, preferred_element_type=F32)


def split(x):
    hi = x.astype(BF16)
    return hi, (x - hi.astype(F32)).astype(BF16)


def mm3(a, b, dims=NN):
    return mm(a[0], b[0], dims) + mm(a[0], b[1], dims) + mm(a[1], b[0], dims)


def selector(lo, length):
    row = lax.broadcasted_iota(jnp.int32, (length, TOK), 0)
    col = lax.broadcasted_iota(jnp.int32, (length, TOK), 1)
    picked = (col // WIN_LON) * SPAN + col % WIN_LON - lo + WIN_LON - 1
    return (row == picked).astype(F32).astype(BF16)


MESH = pl.DeviceIdType.MESH
LATS = 16
LONS = 16
CHIPS = 8


def remote(src, dst, send, recv, target):
    return pltpu.make_async_remote_copy(
        src_ref=src, dst_ref=dst, send_sem=send, recv_sem=recv, device_id=target, device_id_type=MESH)


def every(first, last):
    return pl.loop(first, last, unroll=True)


def main_kernel(
    f_ref, g_ref, gain_ref, wqkv_ref, wout_ref, table_ref,
    out_b, out_g, rows_b, rows_g, cols_b, cols_g, total, table_total,
    ext_f, ext_g,
    xs, ups, inv_s, s_hi, s_lo,
    kcat, vcat, q_hi, q_lo, do_hi, do_lo,
    qt, kt, vt, dot_, bias, dsacc, bias_raw,
    mix, dq, dk, dv, mix_t, sums_ref, chunks, tables,
    half, recv_p, recv_a, recv_t, recv_b, part, tab_raw, o_s,
    local_sem, in_send, in_recv, halo_send, halo_recv, p_send, p_recv, a_send, a_recv,
    t_send, t_recv, b_send, b_recv, c_send, c_recv, d_send, d_recv, m_send, m_recv, e_send, e_recv,
):
    lat = lax.axis_index("lat")
    lon = lax.axis_index("lon")
    chip = lax.div(lat, 2)
    core = lax.rem(lat, 2)
    mate = chip * 2 + 1 - core
    up, down = lax.rem(lat + 1, LATS), lax.rem(lat + LATS - 1, LATS)
    right, left = lax.rem(lon + 1, LONS), lax.rem(lon + LONS - 1, LONS)
    local = []
    for i, (src, dst) in enumerate(((f_ref, ext_f), (g_ref, ext_g))):
        copy = pltpu.make_async_copy(
            src.at[:, pl.ds(3, 9)], dst.at[:, pl.ds(0, 9), pl.ds(0, 48)], local_sem.at[i])
        copy.start()
        local.append(copy)
    barrier = pltpu.get_barrier_semaphore()

    def greet(target):
        pl.semaphore_signal(barrier, inc=1, device_id=target, device_id_type=MESH)

    @every(1, LONS)
    def _(k):
        greet((lat, lax.rem(lon + k, LONS)))

    @every(1, LATS)
    def _(k):
        greet((lax.rem(lat + k, LATS), lon))

    greet((up, right))
    greet((down, left))
    pl.semaphore_wait(barrier, 32)
    halos_in = []
    for i, (src, dst) in enumerate(((f_ref, ext_f), (g_ref, ext_g))):
        pieces = (
            (src.at[:, pl.ds(3, 9), pl.ds(0, 8)], dst.at[:, pl.ds(0, 9), pl.ds(48, 8)], (lat, left)),
            (src.at[:, pl.ds(0, 3), pl.ds(0, 8)], dst.at[:, pl.ds(9, 3), pl.ds(48, 8)], (down, left)),
            (src.at[:, pl.ds(0, 3)], dst.at[:, pl.ds(9, 3), pl.ds(0, 48)], (down, lon)),
        )
        for j, (a, b, target) in enumerate(pieces):
            copy = remote(a, b, in_send.at[i * 3 + j], in_recv.at[i * 3 + j], target)
            copy.start()
            halos_in.append(copy)

    factor = HEAD ** (-0.5)
    gain = gain_ref[...]
    w = wqkv_ref[...]
    wq = w[:, :D] * factor
    wk = w[:, D:2 * D]
    wv = w[:, 2 * D:]

    def replicated(m):
        parts = []
        for h in range(HEADS):
            parts += [m[:, h * HEAD:(h + 1) * HEAD]] * 4
        return jnp.concatenate(parts, axis=1)

    wkr = split(replicated(wk))
    wvr = split(replicated(wv))
    wqs = split(wq)
    wt = split(jnp.concatenate([wq.T, wk.T, wv.T], axis=0))
    wo = split(wout_ref[...])
    wks = split(wk)
    wvs = split(wv)
    wqp = split(w[:, :D])

    for a in range(2):
        for h in range(HEADS):
            for i in range(OUTER):
                at = (a * HEADS + h) * OUTER + i
                tab_raw[at:at + 1, :] = table_ref[h, a:a + 1, i * OUTER * SPAN:(i + 1) * OUTER * SPAN]
    t0 = tab_raw[...]
    t_hi = t0.astype(BF16)
    rest = t0 - t_hi.astype(F32)
    t_mid = rest.astype(BF16)
    t_lo = (rest - t_mid.astype(F32)).astype(BF16)
    for lo in range(WIN_LON):
        sel = selector(lo, OUTER * SPAN)
        bias_raw[:, lo, :] = mm(t_hi, sel) + mm(t_mid, sel) + mm(t_lo, sel)
    row = lax.broadcasted_iota(jnp.int32, (TOK, TOK), 0)
    col = lax.broadcasted_iota(jnp.int32, (TOK, TOK), 1)
    half_r = (row // WIN_LON) % WIN_LAT < WIN_LAT // 2
    half_c = (col // WIN_LON) % WIN_LAT < WIN_LAT // 2
    apart = half_r != half_c
    for a in range(2):
        on_seam = lat * 2 + a == 31
        cut = jnp.logical_and(apart, on_seam)
        for h in range(HEADS):
            g = a * HEADS + h
            b = bias_raw[g * OUTER:(g + 1) * OUTER].reshape(TOK, TOK)
            bias[g] = jnp.where(cut, MASKED, b.T)
            dsacc[g] = jnp.zeros((TOK, TOK), F32)

    def front(first_window, last_window):
        for wi in range(first_window, last_window):
            a, b = divmod(wi, 4)
            for l in range(2):
                for r in range(WIN_LAT):
                    at = wi * TOK + (l * WIN_LAT + r) * WIN_LON
                    c0 = 6 + WIN_LON * b
                    xs[at:at + WIN_LON, :] = ext_f[l, a * WIN_LAT + r, c0:c0 + WIN_LON, :]
                    ups[at:at + WIN_LON, :] = ext_g[l, a * WIN_LAT + r, c0:c0 + WIN_LON, :]

        @pl.loop(first_window, last_window)
        def _(wi):
            rows = pl.ds(pl.multiple_of(wi * TOK, TOK), TOK)
            x = xs[rows, :]
            c = x - jnp.mean(x, axis=-1, keepdims=True)
            inv = lax.rsqrt(jnp.mean(c * c, axis=-1, keepdims=True) + EPSILON)
            n = c * inv
            xs[rows, :] = n
            inv_s[rows, :] = jnp.broadcast_to(inv, (TOK, 128))
            s = split(n * gain)
            s_hi[rows, :] = s[0]
            s_lo[rows, :] = s[1]
            pt = mm3(wt, s, NT)
            for i, ref in enumerate((qt, kt, vt)):
                ph, pll = split(pt[i * D:(i + 1) * D])
                for h in range(HEADS):
                    a_, b_ = ph[h * HEAD:(h + 1) * HEAD], pll[h * HEAD:(h + 1) * HEAD]
                    if ref is qt:
                        ref[wi, h] = jnp.concatenate([a_, b_, a_, b_], axis=0)
                    else:
                        ref[wi, h] = jnp.concatenate([a_, b_], axis=0)
            u = split(ups[rows, :])
            dt = split(mm3(wo, u, NT))
            for h in range(HEADS):
                a_, b_ = dt[0][h * HEAD:(h + 1) * HEAD], dt[1][h * HEAD:(h + 1) * HEAD]
                dot_[wi, h] = jnp.concatenate([a_, b_, a_, b_], axis=0)

        size = (last_window - first_window) * TOK
        rows = slice(first_window * TOK, last_window * TOK)
        first_half = lax.broadcasted_iota(jnp.int32, (size, 256), 1) % 128 < 64
        left_side = (s_hi[rows, :], s_lo[rows, :])
        for j in range(3):
            cols = slice(j * 256, (j + 1) * 256)
            for wr, ref in ((wkr, kcat), (wvr, vcat)):
                ph, pll = split(mm3(left_side, (wr[0][:, cols], wr[1][:, cols])))
                ref[rows, cols] = jnp.where(first_half, ph, pll)
        qh, ql = split(mm3(left_side, wqs))
        q_hi[rows, :] = qh
        q_lo[rows, :] = ql
        dh, dl = split(mm3(split(ups[rows, :]), wo, NT))
        do_hi[rows, :] = dh
        do_lo[rows, :] = dl

    for copy in local:
        copy.wait()
    front(0, 3)
    head_of = lax.broadcasted_iota(jnp.int32, (TOK, D), 1) // HEAD

    @pl.loop(0, WINDOWS)
    def _(wi):
        @pl.when(wi == 3)
        def _():
            for copy in halos_in:
                copy.wait()
            front(3, WINDOWS)

        rows = pl.ds(pl.multiple_of(wi * TOK, TOK), TOK)
        base = lax.div(wi, 4) * HEADS
        dv_acc = jnp.zeros((TOK, D), F32)
        dk_acc = jnp.zeros((TOK, D), F32)
        zero = jnp.zeros((TOK, D), BF16)
        for h in range(HEADS):
            blk = slice(h * 128, (h + 1) * 128)
            st = mm(kcat[rows, blk], qt[wi, h]) + bias[base + h]
            e = jnp.exp(st - jnp.max(st, axis=0, keepdims=True))
            p = e * (1.0 / jnp.sum(e, axis=0, keepdims=True))
            p_hi, p_lo = split(p)
            dp = mm(vcat[rows, blk], dot_[wi, h])
            ds = p * (dp - jnp.sum(p * dp, axis=0, keepdims=True))
            dsacc[base + h] += ds
            ds_hi, ds_lo = split(ds)
            v2 = vt[wi, h]
            m2 = mm(v2, p_hi)
            m = m2[:HEAD] + m2[HEAD:] + mm(v2[:HEAD], p_lo)
            mix_t[h * HEAD:(h + 1) * HEAD, :] = m
            k2 = kt[wi, h]
            g2 = mm(k2, ds_hi)
            g = g2[:HEAD] + g2[HEAD:] + mm(k2[:HEAD], ds_lo)
            dq[wi, h * HEAD:(h + 1) * HEAD, :] = g * factor
            mine = head_of == h
            o_hi = jnp.where(mine, do_hi[rows, :], zero)
            o_lo = jnp.where(mine, do_lo[rows, :], zero)
            dv_acc += mm(p_hi, o_hi) + mm(p_hi, o_lo) + mm(p_lo, o_hi)
            c_hi = jnp.where(mine, q_hi[rows, :], zero)
            c_lo = jnp.where(mine, q_lo[rows, :], zero)
            dk_acc += mm(ds_hi, c_hi) + mm(ds_hi, c_lo) + mm(ds_lo, c_hi)
        dv[rows, :] = dv_acc
        dk[rows, :] = dk_acc
        mix[wi] = mix_t[...]

    def scatter(wi, src, out):
        a, b = divmod(wi, 4)
        for l in range(2):
            for r in range(WIN_LAT):
                at = wi * TOK + (l * WIN_LAT + r) * WIN_LON
                c0 = 6 + WIN_LON * b
                out[l, a * WIN_LAT + r, c0:c0 + WIN_LON, :] = src[at:at + WIN_LON, :]

    def halo_side(i, out, cols):
        return (
            remote(out.at[:, pl.ds(0, 9), pl.ds(48, 8)], cols.at[:, pl.ds(3, 9)],
                   halo_send.at[i * 3], halo_recv.at[i * 3], (lat, right)),
            remote(out.at[:, pl.ds(9, 3), pl.ds(48, 8)], cols.at[:, pl.ds(0, 3)],
                   halo_send.at[i * 3 + 1], halo_recv.at[i * 3 + 1], (up, right)),
        )

    def halo_rows(i, out, edge):
        return (
            remote(out.at[:, pl.ds(9, 3), pl.ds(0, 48)], edge,
                   halo_send.at[i * 3 + 2], halo_recv.at[i * 3 + 2], (up, lon)),
        )

    @pl.loop(0, WINDOWS)
    def _(wi):
        rows = pl.ds(pl.multiple_of(wi * TOK, TOK), TOK)
        o_s[rows, :] = mm3(split(mix[wi].T), wo)

    for wi in range(WINDOWS):
        scatter(wi, o_s, out_b)
    branch_halos = halo_side(0, out_b, cols_b) + halo_rows(0, out_b, rows_b)
    for copy in branch_halos:
        copy.start()

    sums_ref[...] = jnp.zeros_like(sums_ref)

    @pl.loop(0, WINDOWS)
    def _(wi):
        rows = pl.ds(pl.multiple_of(wi * TOK, TOK), TOK)
        nt = split(xs[rows, :].T)
        sums_ref[:, 3 * D:] += mm3(split(mix[wi]), split(ups[rows, :]))
        sums_ref[:, :D] += mm3(nt, split(dq[wi].T))
        sums_ref[:, D:2 * D] += mm3(nt, split(dk[rows, :]))
        sums_ref[:, 2 * D:3 * D] += mm3(nt, split(dv[rows, :]))

    for i in range(24):
        for j in range(6):
            q, s = divmod(i * 6 + j, 9)
            chunks[q // 2, q % 2, s * 8:s * 8 + 8, :] = sums_ref[i * 8:i * 8 + 8, j * 128:(j + 1) * 128]
    pair = remote(chunks.at[:, 1 - core], recv_p, p_send, p_recv, (mate, lon))
    pair.start()

    for g in range(2 * HEADS):
        bias_raw[g * OUTER:(g + 1) * OUTER] = dsacc[g].T.reshape(OUTER, WIN_LON, TOK)
    acc = jnp.zeros((TOK, 384), F32)
    for lo in range(WIN_LON):
        sel = selector(lo, 384)
        d_hi, d_lo = split(bias_raw[:, lo, :])
        acc += mm(d_hi, sel, NT) + mm(d_lo, sel, NT)
    tables[13:16] = jnp.zeros((3, 32, 128), F32)
    for i in range(18):
        for j in range(3):
            q, s = divmod(i * 3 + j, 4)
            tables[q, s * 8:s * 8 + 8, :] = acc[i * 8:i * 8 + 8, j * 128:(j + 1) * 128]

    pair.wait()
    half[...] = chunks[:, core] + recv_p[...]

    def stage_a(k):
        peer = lax.rem(chip + k, CHIPS)
        return remote(half.at[peer], recv_a.at[k - 1], a_send.at[k - 1], a_recv.at[k - 1], (peer * 2 + core, lon))

    @every(1, CHIPS)
    def _(k):
        stage_a(k).start()

    def stage_t(k):
        peer = lax.rem(lon + k, LONS)
        return remote(tables.at[peer], recv_t.at[k - 1], t_send.at[k - 1], t_recv.at[k - 1], (lat, peer))

    @every(1, LONS)
    def _(k):
        stage_t(k).start()

    def rest_of(wi):
        rows = pl.ds(pl.multiple_of(wi * TOK, TOK), TOK)
        n = xs[rows, :]
        grad_scaled = (
            mm3(split(dq[wi].T), wqp, NT) + mm3(split(dk[rows, :]), wks, NT) + mm3(split(dv[rows, :]), wvs, NT)
        )
        g = grad_scaled * gain
        o_s[rows, :] = inv_s[rows, :][:, :1] * (
            g - jnp.mean(g, axis=-1, keepdims=True)
            - n * jnp.mean(g * n, axis=-1, keepdims=True)
        )

    @pl.loop(3, WINDOWS)
    def _(wi):
        rest_of(wi)

    for wi in range(3, WINDOWS):
        scatter(wi, o_s, out_g)

    @every(1, CHIPS)
    def _(k):
        stage_a(k).wait()

    own = half[chip]
    for k in range(CHIPS - 1):
        own += recv_a[k]
    part[...] = own

    def stage_b(k):
        peer = lax.rem(lon + k, LONS)
        at = pl.ds(pl.multiple_of(jnp.minimum(peer, 8) * 8, 8), 8)
        return peer, remote(part.at[at], recv_b.at[k - 1], b_send.at[k - 1], b_recv.at[k - 1], (lat, peer))

    @every(1, LONS)
    def _(k):
        peer, copy = stage_b(k)

        @pl.when(peer < 9)
        def _():
            copy.start()

    grad_rows = halo_rows(1, out_g, rows_g)
    for copy in grad_rows:
        copy.start()

    @pl.loop(0, 3)
    def _(wi):
        rest_of(wi)

    for wi in range(3):
        scatter(wi, o_s, out_g)

    mine = pl.ds(pl.multiple_of(jnp.minimum(lon, 8) * 8, 8), 8)

    def stage_c(k):
        peer = lax.rem(lon + k, LONS)
        here = total.at[chip, core, mine]
        return remote(here, here, c_send.at[k - 1], c_recv.at[k - 1], (lat, peer))

    @pl.when(lon < 9)
    def _():
        @every(1, LONS)
        def _(k):
            stage_b(k)[1].wait_recv()

        tile = part[mine]
        for k in range(LONS - 1):
            tile += recv_b[k]
        total[chip, core, mine] = tile

        @every(1, LONS)
        def _(k):
            stage_c(k).start()

    grad_side = halo_side(1, out_g, cols_g)
    for copy in grad_side:
        copy.start()

    @every(1, LONS)
    def _(k):
        stage_t(k).wait()

    own = tables[lon]
    for k in range(LONS - 1):
        own += recv_t[k]
    table_total[lon] = own

    def stage_e(k):
        peer = lax.rem(lon + k, LONS)
        return remote(table_total.at[lon], table_total.at[lon], e_send.at[k - 1], e_recv.at[k - 1], (lat, peer))

    @every(1, LONS)
    def _(k):
        stage_e(k).start()

    @every(1, LONS)
    def _(k):
        peer = lax.rem(lon + LONS - k, LONS)
        at = pl.ds(pl.multiple_of(jnp.minimum(peer, 8) * 8, 8), 8)

        @pl.when(peer < 9)
        def _():
            there = total.at[chip, core, at]
            remote(there, there, c_send.at[k - 1], c_recv.at[k - 1], (lat, peer)).wait_recv()

    def stage_d(k):
        peer = lax.rem(chip + k, CHIPS)
        here = total.at[chip, core]
        return remote(here, here, d_send.at[k - 1], d_recv.at[k - 1], (peer * 2 + core, lon))

    @every(1, CHIPS)
    def _(k):
        stage_d(k).start()

    @every(1, LONS)
    def _(k):
        peer, copy = stage_b(k)

        @pl.when(peer < 9)
        def _():
            copy.wait_send()

    @pl.when(lon < 9)
    def _():
        @every(1, LONS)
        def _(k):
            stage_c(k).wait_send()

    @every(1, CHIPS)
    def _(k):
        peer = lax.rem(chip + CHIPS - k, CHIPS)
        there = total.at[peer, core]
        remote(there, there, d_send.at[k - 1], d_recv.at[k - 1], (peer * 2 + core, lon)).wait_recv()

    ours = total.at[:, core]
    swap = remote(ours, ours, m_send, m_recv, (mate, lon))
    swap.start()

    @every(1, CHIPS)
    def _(k):
        stage_d(k).wait_send()

    for copy in branch_halos + grad_rows + grad_side:
        copy.wait()

    @every(1, LONS)
    def _(k):
        stage_e(k).wait_send()
        peer = lax.rem(lon + LONS - k, LONS)
        there = table_total.at[peer]
        remote(there, there, e_send.at[k - 1], e_recv.at[k - 1], (lat, peer)).wait_recv()

    swap.wait_send()
    theirs = total.at[:, 1 - core]
    remote(theirs, theirs, m_send, m_recv, (mate, lon)).wait_recv()


def main(fields, cotangent, gain, wqkv, wout, table):
    vm = pl.BlockSpec(memory_space=pltpu.VMEM)
    anywhere = pl.BlockSpec(memory_space=pl.ANY)
    rows = WINDOWS * TOK
    DMA = pltpu.SemaphoreType.DMA
    scratch = [
        pltpu.VMEM((2, 12, 56, D), F32), pltpu.VMEM((2, 12, 56, D), F32),
        pltpu.VMEM((rows, D), F32), pltpu.VMEM((rows, D), F32), pltpu.VMEM((rows, 128), F32),
        pltpu.VMEM((rows, D), BF16), pltpu.VMEM((rows, D), BF16),
        pltpu.VMEM((rows, 768), BF16), pltpu.VMEM((rows, 768), BF16),
        pltpu.VMEM((rows, D), BF16), pltpu.VMEM((rows, D), BF16),
        pltpu.VMEM((rows, D), BF16), pltpu.VMEM((rows, D), BF16),
        pltpu.VMEM((WINDOWS, HEADS, 128, TOK), BF16),
        pltpu.VMEM((WINDOWS, HEADS, 64, TOK), BF16),
        pltpu.VMEM((WINDOWS, HEADS, 64, TOK), BF16),
        pltpu.VMEM((WINDOWS, HEADS, 128, TOK), BF16),
        pltpu.VMEM((2 * HEADS, TOK, TOK), F32),
        pltpu.VMEM((2 * HEADS, TOK, TOK), F32),
        pltpu.VMEM((TOK, WIN_LON, TOK), F32),
        pltpu.VMEM((WINDOWS, D, TOK), F32), pltpu.VMEM((WINDOWS, D, TOK), F32),
        pltpu.VMEM((rows, D), F32), pltpu.VMEM((rows, D), F32),
        pltpu.VMEM((D, TOK), F32),
        pltpu.VMEM((D, 4 * D), F32),
        pltpu.VMEM((8, 2, 72, 128), F32), pltpu.VMEM((16, 32, 128), F32),
        pltpu.VMEM((8, 72, 128), F32), pltpu.VMEM((8, 72, 128), F32), pltpu.VMEM((7, 72, 128), F32),
        pltpu.VMEM((15, 32, 128), F32), pltpu.VMEM((15, 8, 128), F32), pltpu.VMEM((72, 128), F32),
        pltpu.VMEM((TOK, OUTER * SPAN), F32), pltpu.VMEM((rows, D), F32),
        DMA((2,)), DMA((6,)), DMA((6,)), DMA((6,)), DMA((6,)), DMA, DMA, DMA((7,)), DMA((7,)),
        DMA((15,)), DMA((15,)), DMA((15,)), DMA((15,)), DMA((15,)), DMA((15,)),
        DMA((7,)), DMA((7,)), DMA, DMA, DMA((15,)), DMA((15,)),
    ]
    whole = jax.ShapeDtypeStruct((2, 12, 56, D), F32)
    edge = jax.ShapeDtypeStruct((2, 3, 48, D), F32)
    side = jax.ShapeDtypeStruct((2, 12, 8, D), F32)
    return pl.pallas_call(
        main_kernel,
        out_shape=[
            whole, whole, edge, edge, side, side,
            jax.ShapeDtypeStruct((8, 2, 72, 128), F32), jax.ShapeDtypeStruct((16, 32, 128), F32),
        ],
        in_specs=[anywhere] * 2 + [vm] * 4,
        out_specs=[vm] * 8,
        scratch_shapes=scratch,
        compiler_params=pltpu.CompilerParams(
            collective_id=0, has_side_effects=True, vmem_limit_bytes=60 * 1024 * 1024),
    )(fields, cotangent, gain, wqkv, wout, table)


def finish_kernel(
    ext_b, ext_g, rows_b, rows_g, cols_b, cols_g, total, table_total, wqkv_ref, gain_ref,
    branch, grads, gain_out, qkv_out, out_out, table_out, full, flat,
):
    for ext, rows, cols, out in ((ext_b, rows_b, cols_b, branch), (ext_g, rows_g, cols_g, grads)):
        out[:, 0:3] = rows[...]
        out[:, 3:12] = ext[:, 0:9, 0:48, :]
        there = lax.broadcasted_iota(jnp.int32, (2, 12, 8, D), 2) < 6
        out[:, :, 0:8, :] = jnp.where(there, cols[...], out[:, :, 0:8, :])
    scale = 1.0 / math.sqrt(LATS * LONS * WINDOWS * TOK)
    for i in range(24):
        for j in range(6):
            q, s = divmod(i * 6 + j, 9)
            full[i * 8:i * 8 + 8, j * 128:(j + 1) * 128] = total[q // 2, q % 2, s * 8:s * 8 + 8, :] * scale
    raw = full[:, :3 * D]
    summed = jnp.sum(raw * wqkv_ref[...], axis=1, keepdims=True)
    gain_out[...] = jnp.broadcast_to(summed, (D, 128)).T[:1]
    qkv_out[...] = raw * jnp.broadcast_to(gain_ref[...], (8, D)).T[:, :1]
    out_out[...] = full[:, 3 * D:]
    for i in range(18):
        for j in range(3):
            q, s = divmod(i * 3 + j, 4)
            flat[i * 8:i * 8 + 8, j * 128:(j + 1) * 128] = table_total[q, s * 8:s * 8 + 8, :]
    for a in range(2):
        for h in range(HEADS):
            for i in range(OUTER):
                at = (a * HEADS + h) * OUTER + i
                table_out[h, a:a + 1, i * OUTER * SPAN:(i + 1) * OUTER * SPAN] = flat[at:at + 1, :OUTER * SPAN]


def finish(ext_b, ext_g, rows_b, rows_g, cols_b, cols_g, total, table_total, wqkv, gain):
    vm = pl.BlockSpec(memory_space=pltpu.VMEM)
    whole = jax.ShapeDtypeStruct((2, 12, 48, D), F32)
    return pl.pallas_call(
        finish_kernel,
        out_shape=[
            whole, whole, jax.ShapeDtypeStruct((1, D), F32), jax.ShapeDtypeStruct((D, 3 * D), F32),
            jax.ShapeDtypeStruct((D, D), F32), jax.ShapeDtypeStruct((HEADS, 2, OUTER * OUTER * SPAN), F32),
        ],
        in_specs=[vm] * 10,
        out_specs=[vm] * 6,
        scratch_shapes=[pltpu.VMEM((D, 4 * D), F32), pltpu.VMEM((TOK, 384), F32)],
        compiler_params=pltpu.CompilerParams(vmem_limit_bytes=60 * 1024 * 1024),
    )(ext_b, ext_g, rows_b, rows_g, cols_b, cols_g, total, table_total, wqkv, gain)


def on_device(fields, cotangent, norm_gain, qkv_weight, out_weight, bias_table):
    table = jnp.transpose(bias_table, (1, 0, 2))
    win_b, win_g, rows_b, rows_g, cols_b, cols_g, total, table_total = main(
        fields, cotangent, norm_gain.reshape(1, D), qkv_weight, out_weight, table)
    branch, grad_fields, gain, qkv, out, gtable = finish(
        win_b, win_g, rows_b, rows_g, cols_b, cols_g, total, table_total, qkv_weight, norm_gain.reshape(1, D))
    return branch, grad_fields, gain.reshape(D), qkv, out, jnp.transpose(gtable, (1, 0, 2))


def solution(mesh):
    cells = P(None, "lat", "lon", None)
    rows = P("lat", None, None)
    return jax.shard_map(
        on_device,
        mesh=mesh,
        in_specs=(cells, cells, P(), P(), P(), rows),
        out_specs=(cells, cells, P(), P(), P(), rows),
        check_vma=False,
    )
```

```python
import math
import jax
import jax.numpy as jnp
from jax import lax
from jax.experimental import pallas as pl
from jax.experimental.pallas import tpu as pltpu
from jax.sharding import PartitionSpec as P

WIN_LAT = 6
WIN_LON = 12
EPSILON = 1e-05
MASKED = -1000000000.0
HEADS = 6
HEAD = 32
D = 192
TOK = 144
WINDOWS = 8
OUTER = 12
SPAN = 23
F32 = jnp.float32
BF16 = jnp.bfloat16
NN = (((1,), (0,)), ((), ()))
NT = (((1,), (1,)), ((), ()))


def mm(a, b, dims=NN):
    return lax.dot_general(a, b, dims, preferred_element_type=F32)


def split(x):
    hi = x.astype(BF16)
    return hi, (x - hi.astype(F32)).astype(BF16)


def mm3(a, b, dims=NN):
    return mm(a[0], b[0], dims) + mm(a[0], b[1], dims) + mm(a[1], b[0], dims)


def selector(lo, length):
    row = lax.broadcasted_iota(jnp.int32, (length, TOK), 0)
    col = lax.broadcasted_iota(jnp.int32, (length, TOK), 1)
    picked = (col // WIN_LON) * SPAN + col % WIN_LON - lo + WIN_LON - 1
    return (row == picked).astype(F32).astype(BF16)


MESH = pl.DeviceIdType.MESH
LATS = 16
LONS = 16
CHIPS = 8


def remote(src, dst, send, recv, target):
    return pltpu.make_async_remote_copy(
        src_ref=src, dst_ref=dst, send_sem=send, recv_sem=recv, device_id=target, device_id_type=MESH)


def every(first, last):
    return pl.loop(first, last, unroll=True)


def main_kernel(
    f_ref, g_ref, gain_ref, wqkv_ref, wout_ref, table_ref,
    out_b, out_g, rows_b, rows_g, cols_b, cols_g, total, first_total, second_total,
    ext_f, ext_g,
    xs, ups, inv_s, s_hi, s_lo,
    kcat, vcat, q_hi, q_lo, do_hi, do_lo,
    qt, kt, vt, dot_, bias, dsacc, bias_raw,
    mix, dq, dk, dv, mix_t, sums_ref, chunks, first_part, second_part,
    half, recv_p, recv_a, first_recv, second_recv, tab_raw, o_s,
    local_sem, in_send, in_recv, halo_send, halo_recv, p_send, p_recv, a_send, a_recv,
    t_send, t_recv, b_send, b_recv, c_send, c_recv, d_send, d_recv, m_send, m_recv, e_send, e_recv,
):
    lat = lax.axis_index("lat")
    lon = lax.axis_index("lon")
    chip = lax.div(lat, 2)
    core = lax.rem(lat, 2)
    mate = chip * 2 + 1 - core
    up, down = lax.rem(lat + 1, LATS), lax.rem(lat + LATS - 1, LATS)
    right, left = lax.rem(lon + 1, LONS), lax.rem(lon + LONS - 1, LONS)
    local = []
    for i, (src, dst) in enumerate(((f_ref, ext_f), (g_ref, ext_g))):
        copy = pltpu.make_async_copy(
            src.at[:, pl.ds(3, 9)], dst.at[:, pl.ds(0, 9), pl.ds(0, 48)], local_sem.at[i])
        copy.start()
        local.append(copy)
    barrier = pltpu.get_barrier_semaphore()

    def greet(target):
        pl.semaphore_signal(barrier, inc=1, device_id=target, device_id_type=MESH)

    @every(1, LONS)
    def _(k):
        greet((lat, lax.rem(lon + k, LONS)))

    @every(1, LATS)
    def _(k):
        greet((lax.rem(lat + k, LATS), lon))

    greet((up, right))
    greet((down, left))
    pl.semaphore_wait(barrier, 32)
    halos_in = []
    for i, (src, dst) in enumerate(((f_ref, ext_f), (g_ref, ext_g))):
        pieces = (
            (src.at[:, pl.ds(3, 9), pl.ds(0, 8)], dst.at[:, pl.ds(0, 9), pl.ds(48, 8)], (lat, left)),
            (src.at[:, pl.ds(0, 3), pl.ds(0, 8)], dst.at[:, pl.ds(9, 3), pl.ds(48, 8)], (down, left)),
            (src.at[:, pl.ds(0, 3)], dst.at[:, pl.ds(9, 3), pl.ds(0, 48)], (down, lon)),
        )
        for j, (a, b, target) in enumerate(pieces):
            copy = remote(a, b, in_send.at[i * 3 + j], in_recv.at[i * 3 + j], target)
            copy.start()
            halos_in.append(copy)

    factor = HEAD ** (-0.5)
    gain = gain_ref[...]
    w = wqkv_ref[...]
    wq = w[:, :D] * factor
    wk = w[:, D:2 * D]
    wv = w[:, 2 * D:]

    def replicated(m):
        parts = []
        for h in range(HEADS):
            parts += [m[:, h * HEAD:(h + 1) * HEAD]] * 4
        return jnp.concatenate(parts, axis=1)

    wkr = split(replicated(wk))
    wvr = split(replicated(wv))
    wqs = split(wq)
    wt = split(jnp.concatenate([wq.T, wk.T, wv.T], axis=0))
    wo = split(wout_ref[...])
    wks = split(wk)
    wvs = split(wv)
    wqp = split(w[:, :D])

    for a in range(2):
        for h in range(HEADS):
            for i in range(OUTER):
                at = (a * HEADS + h) * OUTER + i
                tab_raw[at:at + 1, :] = table_ref[h, a:a + 1, i * OUTER * SPAN:(i + 1) * OUTER * SPAN]
    t0 = tab_raw[...]
    t_hi = t0.astype(BF16)
    rest = t0 - t_hi.astype(F32)
    t_mid = rest.astype(BF16)
    t_lo = (rest - t_mid.astype(F32)).astype(BF16)
    for lo in range(WIN_LON):
        sel = selector(lo, OUTER * SPAN)
        bias_raw[:, lo, :] = mm(t_hi, sel) + mm(t_mid, sel) + mm(t_lo, sel)
    row = lax.broadcasted_iota(jnp.int32, (TOK, TOK), 0)
    col = lax.broadcasted_iota(jnp.int32, (TOK, TOK), 1)
    half_r = (row // WIN_LON) % WIN_LAT < WIN_LAT // 2
    half_c = (col // WIN_LON) % WIN_LAT < WIN_LAT // 2
    apart = half_r != half_c
    for a in range(2):
        on_seam = lat * 2 + a == 31
        cut = jnp.logical_and(apart, on_seam)
        for h in range(HEADS):
            g = a * HEADS + h
            b = bias_raw[g * OUTER:(g + 1) * OUTER].reshape(TOK, TOK)
            bias[g] = jnp.where(cut, MASKED, b.T)
            dsacc[g] = jnp.zeros((TOK, TOK), F32)

    def front(first_window, last_window):
        for wi in range(first_window, last_window):
            a, b = divmod(wi, 4)
            for l in range(2):
                for r in range(WIN_LAT):
                    at = wi * TOK + (l * WIN_LAT + r) * WIN_LON
                    c0 = 6 + WIN_LON * b
                    xs[at:at + WIN_LON, :] = ext_f[l, a * WIN_LAT + r, c0:c0 + WIN_LON, :]
                    ups[at:at + WIN_LON, :] = ext_g[l, a * WIN_LAT + r, c0:c0 + WIN_LON, :]

        @pl.loop(first_window, last_window)
        def _(wi):
            rows = pl.ds(pl.multiple_of(wi * TOK, TOK), TOK)
            x = xs[rows, :]
            c = x - jnp.mean(x, axis=-1, keepdims=True)
            inv = lax.rsqrt(jnp.mean(c * c, axis=-1, keepdims=True) + EPSILON)
            n = c * inv
            xs[rows, :] = n
            inv_s[rows, :] = jnp.broadcast_to(inv, (TOK, 128))
            s = split(n * gain)
            s_hi[rows, :] = s[0]
            s_lo[rows, :] = s[1]
            pt = mm3(wt, s, NT)
            for i, ref in enumerate((qt, kt, vt)):
                ph, pll = split(pt[i * D:(i + 1) * D])
                for h in range(HEADS):
                    a_, b_ = ph[h * HEAD:(h + 1) * HEAD], pll[h * HEAD:(h + 1) * HEAD]
                    if ref is qt:
                        ref[wi, h] = jnp.concatenate([a_, b_, a_, b_], axis=0)
                    else:
                        ref[wi, h] = jnp.concatenate([a_, b_], axis=0)
            u = split(ups[rows, :])
            dt = split(mm3(wo, u, NT))
            for h in range(HEADS):
                a_, b_ = dt[0][h * HEAD:(h + 1) * HEAD], dt[1][h * HEAD:(h + 1) * HEAD]
                dot_[wi, h] = jnp.concatenate([a_, b_, a_, b_], axis=0)

        size = (last_window - first_window) * TOK
        rows = slice(first_window * TOK, last_window * TOK)
        first_half = lax.broadcasted_iota(jnp.int32, (size, 256), 1) % 128 < 64
        left_side = (s_hi[rows, :], s_lo[rows, :])
        for j in range(3):
            cols = slice(j * 256, (j + 1) * 256)
            for wr, ref in ((wkr, kcat), (wvr, vcat)):
                ph, pll = split(mm3(left_side, (wr[0][:, cols], wr[1][:, cols])))
                ref[rows, cols] = jnp.where(first_half, ph, pll)
        qh, ql = split(mm3(left_side, wqs))
        q_hi[rows, :] = qh
        q_lo[rows, :] = ql
        dh, dl = split(mm3(split(ups[rows, :]), wo, NT))
        do_hi[rows, :] = dh
        do_lo[rows, :] = dl

    for copy in local:
        copy.wait()
    front(0, 3)
    class LonSum:
        def __init__(self, src, recv, out, s1, r1, s2, r2):
            self.refs = src, recv, out, s1, r1, s2, r2

        def scatter_copy(self, k):
            src, recv, out, s1, r1, s2, r2 = self.refs
            peer = lax.rem(lon + k, LONS)
            return remote(src.at[peer], recv.at[k - 1], s1.at[k - 1], r1.at[k - 1], (lat, peer))

        def gather_copy(self, k, owner, peer):
            src, recv, out, s1, r1, s2, r2 = self.refs
            return remote(out.at[owner], out.at[owner], s2.at[k - 1], r2.at[k - 1], (lat, peer))

        def start(self):
            @every(1, LONS)
            def _(k):
                self.scatter_copy(k).start()

        def middle(self):
            src, recv, out = self.refs[:3]

            @every(1, LONS)
            def _(k):
                self.scatter_copy(k).wait()

            own = src[lon]
            for k in range(LONS - 1):
                own += recv[k]
            out[lon] = own

            @every(1, LONS)
            def _(k):
                self.gather_copy(k, lon, lax.rem(lon + k, LONS)).start()

        def end(self):
            @every(1, LONS)
            def _(k):
                self.gather_copy(k, lon, lax.rem(lon + k, LONS)).wait_send()
                owner = lax.rem(lon + LONS - k, LONS)
                self.gather_copy(k, owner, owner).wait_recv()

    first = LonSum(first_part, first_recv, first_total, t_send, t_recv, e_send, e_recv)
    second = LonSum(second_part, second_recv, second_total, b_send, b_recv, c_send, c_recv)

    def place(ref, t, value):
        q, s = divmod(t, 2)
        ref[q, s * 8:s * 8 + 8, :] = value

    def table_gradient(a, ref):
        for g in range(a * HEADS, (a + 1) * HEADS):
            bias_raw[g * OUTER:(g + 1) * OUTER] = dsacc[g].T.reshape(OUTER, WIN_LON, TOK)
        acc = jnp.zeros((72, 384), F32)
        for lo in range(WIN_LON):
            sel = selector(lo, 384)
            d_hi, d_lo = split(bias_raw[a * 72:(a + 1) * 72, lo, :])
            acc += mm(d_hi, sel, NT) + mm(d_lo, sel, NT)
        for i in range(9):
            for j in range(2):
                place(ref, i * 2 + j, acc[i * 8:i * 8 + 8, j * 128:(j + 1) * 128])
        for p, members in enumerate((range(6), range(6, 9))):
            packed = jnp.zeros((8, 128), F32)
            for i in members:
                tail = acc[i * 8:i * 8 + 8, 256:]
                turn = 20 * (i % 6)
                packed += tail if turn == 0 else pltpu.roll(tail, turn, 1)
            place(ref, 18 + p, packed)

    def scatter(wi, src, out):
        a, b = divmod(wi, 4)
        for l in range(2):
            for r in range(WIN_LAT):
                at = wi * TOK + (l * WIN_LAT + r) * WIN_LON
                c0 = 6 + WIN_LON * b
                out[l, a * WIN_LAT + r, c0:c0 + WIN_LON, :] = src[at:at + WIN_LON, :]

    def halo_copy(i, j, src, dst, target):
        return remote(src, dst, halo_send.at[i * 4 + j], halo_recv.at[i * 4 + j], target)

    def halo_first(i, out, cols):
        return halo_copy(i, 0, out.at[:, pl.ds(0, 6), pl.ds(48, 8)], cols.at[:, pl.ds(3, 6)], (lat, right))

    def halo_second(i, out, cols):
        return halo_copy(i, 1, out.at[:, pl.ds(6, 3), pl.ds(48, 8)], cols.at[:, pl.ds(9, 3)], (lat, right))

    def halo_corner(i, out, cols):
        return halo_copy(i, 2, out.at[:, pl.ds(9, 3), pl.ds(48, 8)], cols.at[:, pl.ds(0, 3)], (up, right))

    def halo_rows(i, out, edge):
        return halo_copy(i, 3, out.at[:, pl.ds(9, 3), pl.ds(0, 48)], edge, (up, lon))

    def branch_of(wi):
        rows = pl.ds(pl.multiple_of(wi * TOK, TOK), TOK)
        o_s[rows, :] = mm3(split(mix[wi].T), wo)

    for i in range(10, 16):
        first_part[i] = jnp.zeros((16, 128), F32)
    second_part[14, 8:16, :] = jnp.zeros((8, 128), F32)
    second_part[15] = jnp.zeros((16, 128), F32)

    head_of = lax.broadcasted_iota(jnp.int32, (TOK, D), 1) // HEAD

    @pl.loop(0, WINDOWS)
    def _(wi):
        @pl.when(wi == 3)
        def _():
            for copy in halos_in:
                copy.wait()
            front(3, WINDOWS)

        @pl.when(wi == 4)
        def _():
            table_gradient(0, first_part)
            first.start()
            pl.loop(0, 4)(branch_of)
            for w in range(4):
                scatter(w, o_s, out_b)
            halo_first(0, out_b, cols_b).start()

        @pl.when(wi == 7)
        def _():
            first.middle()

        rows = pl.ds(pl.multiple_of(wi * TOK, TOK), TOK)
        base = lax.div(wi, 4) * HEADS
        dv_acc = jnp.zeros((TOK, D), F32)
        dk_acc = jnp.zeros((TOK, D), F32)
        zero = jnp.zeros((TOK, D), BF16)
        for h in range(HEADS):
            blk = slice(h * 128, (h + 1) * 128)
            st = mm(kcat[rows, blk], qt[wi, h]) + bias[base + h]
            e = jnp.exp(st - jnp.max(st, axis=0, keepdims=True))
            p = e * (1.0 / jnp.sum(e, axis=0, keepdims=True))
            p_hi, p_lo = split(p)
            dp = mm(vcat[rows, blk], dot_[wi, h])
            ds = p * (dp - jnp.sum(p * dp, axis=0, keepdims=True))
            dsacc[base + h] += ds
            ds_hi, ds_lo = split(ds)
            v2 = vt[wi, h]
            m2 = mm(v2, p_hi)
            m = m2[:HEAD] + m2[HEAD:] + mm(v2[:HEAD], p_lo)
            mix_t[h * HEAD:(h + 1) * HEAD, :] = m
            k2 = kt[wi, h]
            g2 = mm(k2, ds_hi)
            g = g2[:HEAD] + g2[HEAD:] + mm(k2[:HEAD], ds_lo)
            dq[wi, h * HEAD:(h + 1) * HEAD, :] = g * factor
            mine = head_of == h
            o_hi = jnp.where(mine, do_hi[rows, :], zero)
            o_lo = jnp.where(mine, do_lo[rows, :], zero)
            dv_acc += mm(p_hi, o_hi) + mm(p_hi, o_lo) + mm(p_lo, o_hi)
            c_hi = jnp.where(mine, q_hi[rows, :], zero)
            c_lo = jnp.where(mine, q_lo[rows, :], zero)
            dk_acc += mm(ds_hi, c_hi) + mm(ds_hi, c_lo) + mm(ds_lo, c_hi)
        dv[rows, :] = dv_acc
        dk[rows, :] = dk_acc
        mix[wi] = mix_t[...]

    pl.loop(4, WINDOWS)(branch_of)
    for wi in range(4, WINDOWS):
        scatter(wi, o_s, out_b)
    halo_second(0, out_b, cols_b).start()
    halo_corner(0, out_b, cols_b).start()
    halo_rows(0, out_b, rows_b).start()

    sums_ref[...] = jnp.zeros_like(sums_ref)

    @pl.loop(0, WINDOWS)
    def _(wi):
        rows = pl.ds(pl.multiple_of(wi * TOK, TOK), TOK)
        nt = split(xs[rows, :].T)
        sums_ref[:, 3 * D:] += mm3(split(mix[wi]), split(ups[rows, :]))
        sums_ref[:, :D] += mm3(nt, split(dq[wi].T))
        sums_ref[:, D:2 * D] += mm3(nt, split(dk[rows, :]))
        sums_ref[:, 2 * D:3 * D] += mm3(nt, split(dv[rows, :]))

    for i in range(24):
        for j in range(6):
            q, s = divmod(i * 6 + j, 9)
            chunks[q // 2, q % 2, s * 8:s * 8 + 8, :] = sums_ref[i * 8:i * 8 + 8, j * 128:(j + 1) * 128]
    pair = remote(chunks.at[:, 1 - core], recv_p, p_send, p_recv, (mate, lon))
    pair.start()

    table_gradient(1, second_part)
    pair.wait()
    half[...] = chunks[:, core] + recv_p[...]

    def stage_a(k):
        peer = lax.rem(chip + k, CHIPS)
        return remote(half.at[peer], recv_a.at[k - 1], a_send.at[k - 1], a_recv.at[k - 1], (peer * 2 + core, lon))

    @every(1, CHIPS)
    def _(k):
        stage_a(k).start()

    def rest_of(wi):
        rows = pl.ds(pl.multiple_of(wi * TOK, TOK), TOK)
        n = xs[rows, :]
        grad_scaled = (
            mm3(split(dq[wi].T), wqp, NT) + mm3(split(dk[rows, :]), wks, NT) + mm3(split(dv[rows, :]), wvs, NT)
        )
        g = grad_scaled * gain
        o_s[rows, :] = inv_s[rows, :][:, :1] * (
            g - jnp.mean(g, axis=-1, keepdims=True)
            - n * jnp.mean(g * n, axis=-1, keepdims=True)
        )

    pl.loop(4, WINDOWS)(rest_of)
    for wi in range(4, WINDOWS):
        scatter(wi, o_s, out_g)

    @every(1, CHIPS)
    def _(k):
        stage_a(k).wait()

    own = half[chip]
    for k in range(CHIPS - 1):
        own += recv_a[k]
    for t in range(9):
        place(second_part, 20 + t, own[t * 8:t * 8 + 8])
    second.start()
    halo_rows(1, out_g, rows_g).start()

    pl.loop(0, 4)(rest_of)
    for wi in range(4):
        scatter(wi, o_s, out_g)

    second.middle()
    halo_first(1, out_g, cols_g).start()
    halo_second(1, out_g, cols_g).start()
    halo_corner(1, out_g, cols_g).start()
    first.end()
    second.end()
    total[chip, core] = second_total[10:15]

    def stage_d(k, owner, peer):
        here = total.at[owner, core]
        return remote(here, here, d_send.at[k - 1], d_recv.at[k - 1], (peer * 2 + core, lon))

    @every(1, CHIPS)
    def _(k):
        stage_d(k, chip, lax.rem(chip + k, CHIPS)).start()

    @every(1, CHIPS)
    def _(k):
        owner = lax.rem(chip + CHIPS - k, CHIPS)
        stage_d(k, owner, owner).wait_recv()

    ours = total.at[:, core]
    swap = remote(ours, ours, m_send, m_recv, (mate, lon))
    swap.start()

    @every(1, CHIPS)
    def _(k):
        stage_d(k, chip, lax.rem(chip + k, CHIPS)).wait_send()

    for i, (out, edge, cols) in enumerate(((out_b, rows_b, cols_b), (out_g, rows_g, cols_g))):
        halo_rows(i, out, edge).wait()
        halo_first(i, out, cols).wait()
        halo_second(i, out, cols).wait()
        halo_corner(i, out, cols).wait()

    swap.wait_send()
    theirs = total.at[:, 1 - core]
    remote(theirs, theirs, m_send, m_recv, (mate, lon)).wait_recv()


def main(fields, cotangent, gain, wqkv, wout, table):
    vm = pl.BlockSpec(memory_space=pltpu.VMEM)
    anywhere = pl.BlockSpec(memory_space=pl.ANY)
    rows = WINDOWS * TOK
    DMA = pltpu.SemaphoreType.DMA
    scratch = [
        pltpu.VMEM((2, 12, 56, D), F32), pltpu.VMEM((2, 12, 56, D), F32),
        pltpu.VMEM((rows, D), F32), pltpu.VMEM((rows, D), F32), pltpu.VMEM((rows, 128), F32),
        pltpu.VMEM((rows, D), BF16), pltpu.VMEM((rows, D), BF16),
        pltpu.VMEM((rows, 768), BF16), pltpu.VMEM((rows, 768), BF16),
        pltpu.VMEM((rows, D), BF16), pltpu.VMEM((rows, D), BF16),
        pltpu.VMEM((rows, D), BF16), pltpu.VMEM((rows, D), BF16),
        pltpu.VMEM((WINDOWS, HEADS, 128, TOK), BF16),
        pltpu.VMEM((WINDOWS, HEADS, 64, TOK), BF16),
        pltpu.VMEM((WINDOWS, HEADS, 64, TOK), BF16),
        pltpu.VMEM((WINDOWS, HEADS, 128, TOK), BF16),
        pltpu.VMEM((2 * HEADS, TOK, TOK), F32),
        pltpu.VMEM((2 * HEADS, TOK, TOK), F32),
        pltpu.VMEM((TOK, WIN_LON, TOK), F32),
        pltpu.VMEM((WINDOWS, D, TOK), F32), pltpu.VMEM((WINDOWS, D, TOK), F32),
        pltpu.VMEM((rows, D), F32), pltpu.VMEM((rows, D), F32),
        pltpu.VMEM((D, TOK), F32),
        pltpu.VMEM((D, 4 * D), F32),
        pltpu.VMEM((8, 2, 72, 128), F32), pltpu.VMEM((16, 16, 128), F32), pltpu.VMEM((16, 16, 128), F32),
        pltpu.VMEM((8, 72, 128), F32), pltpu.VMEM((8, 72, 128), F32), pltpu.VMEM((7, 72, 128), F32),
        pltpu.VMEM((15, 16, 128), F32), pltpu.VMEM((15, 16, 128), F32),
        pltpu.VMEM((TOK, OUTER * SPAN), F32), pltpu.VMEM((rows, D), F32),
        DMA((2,)), DMA((6,)), DMA((6,)), DMA((8,)), DMA((8,)), DMA, DMA, DMA((7,)), DMA((7,)),
        DMA((15,)), DMA((15,)), DMA((15,)), DMA((15,)), DMA((15,)), DMA((15,)),
        DMA((7,)), DMA((7,)), DMA, DMA, DMA((15,)), DMA((15,)),
    ]
    whole = jax.ShapeDtypeStruct((2, 12, 56, D), F32)
    edge = jax.ShapeDtypeStruct((2, 3, 48, D), F32)
    side = jax.ShapeDtypeStruct((2, 12, 8, D), F32)
    return pl.pallas_call(
        main_kernel,
        out_shape=[
            whole, whole, edge, edge, side, side,
            jax.ShapeDtypeStruct((8, 2, 5, 16, 128), F32),
            jax.ShapeDtypeStruct((16, 16, 128), F32), jax.ShapeDtypeStruct((16, 16, 128), F32),
        ],
        in_specs=[anywhere] * 2 + [vm] * 4,
        out_specs=[vm] * 9,
        scratch_shapes=scratch,
        compiler_params=pltpu.CompilerParams(
            collective_id=0, has_side_effects=True, vmem_limit_bytes=60 * 1024 * 1024),
    )(fields, cotangent, gain, wqkv, wout, table)


def finish_kernel(
    ext_b, ext_g, rows_b, rows_g, cols_b, cols_g, total, first_total, second_total, wqkv_ref, gain_ref,
    branch, grads, gain_out, qkv_out, out_out, table_out, full, flat,
):
    for ext, rows, cols, out in ((ext_b, rows_b, cols_b, branch), (ext_g, rows_g, cols_g, grads)):
        out[:, 0:3] = rows[...]
        out[:, 3:12] = ext[:, 0:9, 0:48, :]
        there = lax.broadcasted_iota(jnp.int32, (2, 12, 8, D), 2) < 6
        out[:, :, 0:8, :] = jnp.where(there, cols[...], out[:, :, 0:8, :])
    scale = 1.0 / math.sqrt(LATS * LONS * WINDOWS * TOK)
    for i in range(24):
        for j in range(6):
            q, s = divmod(i * 6 + j, 9)
            full[i * 8:i * 8 + 8, j * 128:(j + 1) * 128] = total[q // 2, q % 2, s // 2, s % 2 * 8:s % 2 * 8 + 8, :] * scale
    raw = full[:, :3 * D]
    summed = jnp.sum(raw * wqkv_ref[...], axis=1, keepdims=True)
    gain_out[...] = jnp.broadcast_to(summed, (D, 128)).T[:1]
    qkv_out[...] = raw * jnp.broadcast_to(gain_ref[...], (8, D)).T[:, :1]
    out_out[...] = full[:, 3 * D:]
    def tile(ref, t):
        q, s = divmod(t, 2)
        return ref[q, s * 8:s * 8 + 8, :]

    for a, ref in enumerate((first_total, second_total)):
        for i in range(9):
            at = a * 72 + i * 8
            for j in range(2):
                flat[at:at + 8, j * 128:(j + 1) * 128] = tile(ref, i * 2 + j)
            packed = tile(ref, 18 + i // 6)
            turn = 20 * (i % 6)
            flat[at:at + 8, 256:384] = packed if turn == 0 else pltpu.roll(packed, 128 - turn, 1)
    for a in range(2):
        for h in range(HEADS):
            for i in range(OUTER):
                at = (a * HEADS + h) * OUTER + i
                table_out[h, a:a + 1, i * OUTER * SPAN:(i + 1) * OUTER * SPAN] = flat[at:at + 1, :OUTER * SPAN]


def finish(ext_b, ext_g, rows_b, rows_g, cols_b, cols_g, total, first_total, second_total, wqkv, gain):
    vm = pl.BlockSpec(memory_space=pltpu.VMEM)
    whole = jax.ShapeDtypeStruct((2, 12, 48, D), F32)
    return pl.pallas_call(
        finish_kernel,
        out_shape=[
            whole, whole, jax.ShapeDtypeStruct((1, D), F32), jax.ShapeDtypeStruct((D, 3 * D), F32),
            jax.ShapeDtypeStruct((D, D), F32), jax.ShapeDtypeStruct((HEADS, 2, OUTER * OUTER * SPAN), F32),
        ],
        in_specs=[vm] * 11,
        out_specs=[vm] * 6,
        scratch_shapes=[pltpu.VMEM((D, 4 * D), F32), pltpu.VMEM((TOK, 384), F32)],
        compiler_params=pltpu.CompilerParams(vmem_limit_bytes=60 * 1024 * 1024),
    )(ext_b, ext_g, rows_b, rows_g, cols_b, cols_g, total, first_total, second_total, wqkv, gain)


def on_device(fields, cotangent, norm_gain, qkv_weight, out_weight, bias_table):
    table = jnp.transpose(bias_table, (1, 0, 2))
    win_b, win_g, rows_b, rows_g, cols_b, cols_g, total, first_total, second_total = main(
        fields, cotangent, norm_gain.reshape(1, D), qkv_weight, out_weight, table)
    branch, grad_fields, gain, qkv, out, gtable = finish(
        win_b, win_g, rows_b, rows_g, cols_b, cols_g, total, first_total, second_total, qkv_weight, norm_gain.reshape(1, D))
    return branch, grad_fields, gain.reshape(D), qkv, out, jnp.transpose(gtable, (1, 0, 2))


def solution(mesh):
    cells = P(None, "lat", "lon", None)
    rows = P("lat", None, None)
    return jax.shard_map(
        on_device,
        mesh=mesh,
        in_specs=(cells, cells, P(), P(), P(), rows),
        out_specs=(cells, cells, P(), P(), P(), rows),
        check_vma=False,
    )
```

```python
import math
import jax
import jax.numpy as jnp
from jax import lax
from jax.experimental import pallas as pl
from jax.experimental.pallas import tpu as pltpu
from jax.sharding import PartitionSpec as P

WIN_LAT = 6
WIN_LON = 12
EPSILON = 1e-05
MASKED = -1000000000.0
HEADS = 6
HEAD = 32
D = 192
TOK = 144
WINDOWS = 8
OUTER = 12
SPAN = 23
F32 = jnp.float32
BF16 = jnp.bfloat16
NN = (((1,), (0,)), ((), ()))
NT = (((1,), (1,)), ((), ()))


def mm(a, b, dims=NN):
    return lax.dot_general(a, b, dims, preferred_element_type=F32)


def split(x):
    hi = x.astype(BF16)
    return hi, (x - hi.astype(F32)).astype(BF16)


def mm3(a, b, dims=NN):
    return mm(a[0], b[0], dims) + mm(a[0], b[1], dims) + mm(a[1], b[0], dims)


def selector(lo, length):
    row = lax.broadcasted_iota(jnp.int32, (length, TOK), 0)
    col = lax.broadcasted_iota(jnp.int32, (length, TOK), 1)
    picked = (col // WIN_LON) * SPAN + col % WIN_LON - lo + WIN_LON - 1
    return (row == picked).astype(F32).astype(BF16)


MESH = pl.DeviceIdType.MESH
LATS = 16
LONS = 16
CHIPS = 8


def remote(src, dst, send, recv, target):
    return pltpu.make_async_remote_copy(
        src_ref=src, dst_ref=dst, send_sem=send, recv_sem=recv, device_id=target, device_id_type=MESH)


def every(first, last):
    return pl.loop(first, last, unroll=True)


def main_kernel(
    f_ref, g_ref, gain_ref, wqkv_ref, wout_ref, table_ref,
    own_b, own_g, rows_b, rows_g, cols_b, cols_g, total, first_total, second_total,
    ext_f, ext_g, out_b, out_g,
    xs, ups, inv_s, s_hi, s_lo,
    kcat, vcat, q_hi, q_lo, do_hi, do_lo,
    qt, kt, vt, dot_, bias, dsacc, bias_raw,
    mix, dq, dk, dv, mix_t, sums_ref, chunks, first_part, second_part,
    half, recv_p, recv_a, z_all, first_recv, second_recv, tab_raw, o_s,
    local_sem, own_sem, in_send, in_recv, halo_send, halo_recv, p_send, p_recv, a_send, a_recv,
    t_send, t_recv, b_send, b_recv, c_send, c_recv, d_send, d_recv, m_send, m_recv, e_send, e_recv, z_send, z_recv,
):
    lat = lax.axis_index("lat")
    lon = lax.axis_index("lon")
    chip = lax.div(lat, 2)
    core = lax.rem(lat, 2)
    mate = chip * 2 + 1 - core
    y_hi = lax.rem(lon, 2)
    z = lax.div(lon, 2)
    plane = chip * 2 + y_hi
    up, down = lax.rem(lat + 1, LATS), lax.rem(lat + LATS - 1, LATS)
    right, left = lax.rem(lon + 1, LONS), lax.rem(lon + LONS - 1, LONS)
    local = []
    for i, (src, dst) in enumerate(((f_ref, ext_f), (g_ref, ext_g))):
        copy = pltpu.make_async_copy(
            src.at[:, pl.ds(3, 9)], dst.at[:, pl.ds(0, 9), pl.ds(0, 48)], local_sem.at[i])
        copy.start()
        local.append(copy)
    barrier = pltpu.get_barrier_semaphore()

    def greet(target):
        pl.semaphore_signal(barrier, inc=1, device_id=target, device_id_type=MESH)

    @every(1, LONS)
    def _(k):
        greet((lat, lax.rem(lon + k, LONS)))

    @every(1, CHIPS)
    def _(k):
        other = lax.rem(chip + k, CHIPS) * 2 + core
        greet((other, z * 2))
        greet((other, z * 2 + 1))

    greet((up, lon))
    greet((down, lon))
    greet((up, right))
    greet((down, left))
    pl.semaphore_wait(barrier, 33)
    halos_in = []
    for i, (src, dst) in enumerate(((f_ref, ext_f), (g_ref, ext_g))):
        pieces = (
            (src.at[:, pl.ds(3, 9), pl.ds(0, 8)], dst.at[:, pl.ds(0, 9), pl.ds(48, 8)], (lat, left)),
            (src.at[:, pl.ds(0, 3), pl.ds(0, 8)], dst.at[:, pl.ds(9, 3), pl.ds(48, 8)], (down, left)),
            (src.at[:, pl.ds(0, 3)], dst.at[:, pl.ds(9, 3), pl.ds(0, 48)], (down, lon)),
        )
        for j, (a, b, target) in enumerate(pieces):
            copy = remote(a, b, in_send.at[i * 3 + j], in_recv.at[i * 3 + j], target)
            copy.start()
            halos_in.append(copy)

    factor = HEAD ** (-0.5)
    gain = gain_ref[...]
    w = wqkv_ref[...]
    wq = w[:, :D] * factor
    wk = w[:, D:2 * D]
    wv = w[:, 2 * D:]

    def replicated(m):
        parts = []
        for h in range(HEADS):
            parts += [m[:, h * HEAD:(h + 1) * HEAD]] * 4
        return jnp.concatenate(parts, axis=1)

    wkr = split(replicated(wk))
    wvr = split(replicated(wv))
    wqs = split(wq)
    wt = split(jnp.concatenate([wq.T, wk.T, wv.T], axis=0))
    wo = split(wout_ref[...])
    wks = split(wk)
    wvs = split(wv)
    wqp = split(w[:, :D])

    for a in range(2):
        for h in range(HEADS):
            for i in range(OUTER):
                at = (a * HEADS + h) * OUTER + i
                tab_raw[at:at + 1, :] = table_ref[h, a:a + 1, i * OUTER * SPAN:(i + 1) * OUTER * SPAN]
    t0 = tab_raw[...]
    t_hi = t0.astype(BF16)
    rest = t0 - t_hi.astype(F32)
    t_mid = rest.astype(BF16)
    t_lo = (rest - t_mid.astype(F32)).astype(BF16)
    for lo in range(WIN_LON):
        sel = selector(lo, OUTER * SPAN)
        bias_raw[:, lo, :] = mm(t_hi, sel) + mm(t_mid, sel) + mm(t_lo, sel)
    row = lax.broadcasted_iota(jnp.int32, (TOK, TOK), 0)
    col = lax.broadcasted_iota(jnp.int32, (TOK, TOK), 1)
    half_r = (row // WIN_LON) % WIN_LAT < WIN_LAT // 2
    half_c = (col // WIN_LON) % WIN_LAT < WIN_LAT // 2
    apart = half_r != half_c
    for a in range(2):
        on_seam = lat * 2 + a == 31
        cut = jnp.logical_and(apart, on_seam)
        for h in range(HEADS):
            g = a * HEADS + h
            b = bias_raw[g * OUTER:(g + 1) * OUTER].reshape(TOK, TOK)
            bias[g] = jnp.where(cut, MASKED, b.T)
            dsacc[g] = jnp.zeros((TOK, TOK), F32)

    def front(first_window, last_window):
        for wi in range(first_window, last_window):
            a, b = divmod(wi, 4)
            for l in range(2):
                for r in range(WIN_LAT):
                    at = wi * TOK + (l * WIN_LAT + r) * WIN_LON
                    c0 = 6 + WIN_LON * b
                    xs[at:at + WIN_LON, :] = ext_f[l, a * WIN_LAT + r, c0:c0 + WIN_LON, :]
                    ups[at:at + WIN_LON, :] = ext_g[l, a * WIN_LAT + r, c0:c0 + WIN_LON, :]

        @pl.loop(first_window, last_window)
        def _(wi):
            rows = pl.ds(pl.multiple_of(wi * TOK, TOK), TOK)
            x = xs[rows, :]
            c = x - jnp.mean(x, axis=-1, keepdims=True)
            inv = lax.rsqrt(jnp.mean(c * c, axis=-1, keepdims=True) + EPSILON)
            n = c * inv
            xs[rows, :] = n
            inv_s[rows, :] = jnp.broadcast_to(inv, (TOK, 128))
            s = split(n * gain)
            s_hi[rows, :] = s[0]
            s_lo[rows, :] = s[1]
            pt = mm3(wt, s, NT)
            for i, ref in enumerate((qt, kt, vt)):
                ph, pll = split(pt[i * D:(i + 1) * D])
                for h in range(HEADS):
                    a_, b_ = ph[h * HEAD:(h + 1) * HEAD], pll[h * HEAD:(h + 1) * HEAD]
                    if ref is qt:
                        ref[wi, h] = jnp.concatenate([a_, b_, a_, b_], axis=0)
                    else:
                        ref[wi, h] = jnp.concatenate([a_, b_], axis=0)
            u = split(ups[rows, :])
            dt = split(mm3(wo, u, NT))
            for h in range(HEADS):
                a_, b_ = dt[0][h * HEAD:(h + 1) * HEAD], dt[1][h * HEAD:(h + 1) * HEAD]
                dot_[wi, h] = jnp.concatenate([a_, b_, a_, b_], axis=0)

        size = (last_window - first_window) * TOK
        rows = slice(first_window * TOK, last_window * TOK)
        first_half = lax.broadcasted_iota(jnp.int32, (size, 256), 1) % 128 < 64
        left_side = (s_hi[rows, :], s_lo[rows, :])
        for j in range(3):
            cols = slice(j * 256, (j + 1) * 256)
            for wr, ref in ((wkr, kcat), (wvr, vcat)):
                ph, pll = split(mm3(left_side, (wr[0][:, cols], wr[1][:, cols])))
                ref[rows, cols] = jnp.where(first_half, ph, pll)
        qh, ql = split(mm3(left_side, wqs))
        q_hi[rows, :] = qh
        q_lo[rows, :] = ql
        dh, dl = split(mm3(split(ups[rows, :]), wo, NT))
        do_hi[rows, :] = dh
        do_lo[rows, :] = dl

    for copy in local:
        copy.wait()
    front(0, 3)
    class LonSum:
        def __init__(self, src, recv, out, s1, r1, s2, r2):
            self.refs = src, recv, out, s1, r1, s2, r2

        def scatter_copy(self, k):
            src, recv, out, s1, r1, s2, r2 = self.refs
            peer = lax.rem(lon + k, LONS)
            return remote(src.at[peer], recv.at[k - 1], s1.at[k - 1], r1.at[k - 1], (lat, peer))

        def gather_copy(self, k, owner, peer):
            src, recv, out, s1, r1, s2, r2 = self.refs
            return remote(out.at[owner], out.at[owner], s2.at[k - 1], r2.at[k - 1], (lat, peer))

        def start(self):
            @every(1, LONS)
            def _(k):
                self.scatter_copy(k).start()

        def middle(self):
            src, recv, out = self.refs[:3]

            @every(1, LONS)
            def _(k):
                self.scatter_copy(k).wait()

            own = src[lon]
            for k in range(LONS - 1):
                own += recv[k]
            out[lon] = own

            @every(1, LONS)
            def _(k):
                self.gather_copy(k, lon, lax.rem(lon + k, LONS)).start()

        def end(self):
            @every(1, LONS)
            def _(k):
                self.gather_copy(k, lon, lax.rem(lon + k, LONS)).wait_send()
                owner = lax.rem(lon + LONS - k, LONS)
                self.gather_copy(k, owner, owner).wait_recv()

    first = LonSum(first_part, first_recv, first_total, t_send, t_recv, e_send, e_recv)
    second = LonSum(second_part, second_recv, second_total, b_send, b_recv, c_send, c_recv)

    def place(ref, t, value):
        q, s = divmod(t, 2)
        ref[q, s * 8:s * 8 + 8, :] = value

    def table_gradient(a, ref):
        for g in range(a * HEADS, (a + 1) * HEADS):
            bias_raw[g * OUTER:(g + 1) * OUTER] = dsacc[g].T.reshape(OUTER, WIN_LON, TOK)
        acc = jnp.zeros((72, 384), F32)
        for lo in range(WIN_LON):
            sel = selector(lo, 384)
            d_hi, d_lo = split(bias_raw[a * 72:(a + 1) * 72, lo, :])
            acc += mm(d_hi, sel, NT) + mm(d_lo, sel, NT)
        for i in range(9):
            for j in range(2):
                place(ref, i * 2 + j, acc[i * 8:i * 8 + 8, j * 128:(j + 1) * 128])
        for p, members in enumerate((range(6), range(6, 9))):
            packed = jnp.zeros((8, 128), F32)
            for i in members:
                tail = acc[i * 8:i * 8 + 8, 256:]
                turn = 20 * (i % 6)
                packed += tail if turn == 0 else pltpu.roll(tail, turn, 1)
            place(ref, 18 + p, packed)

    def scatter(wi, src, out):
        a, b = divmod(wi, 4)
        for l in range(2):
            for r in range(WIN_LAT):
                at = wi * TOK + (l * WIN_LAT + r) * WIN_LON
                c0 = 6 + WIN_LON * b
                out[l, a * WIN_LAT + r, c0:c0 + WIN_LON, :] = src[at:at + WIN_LON, :]

    def halo_copy(i, j, src, dst, target):
        return remote(src, dst, halo_send.at[i * 4 + j], halo_recv.at[i * 4 + j], target)

    def halo_first(i, out, cols):
        return halo_copy(i, 0, out.at[:, pl.ds(0, 6), pl.ds(48, 8)], cols.at[:, pl.ds(3, 6)], (lat, right))

    def halo_second(i, out, cols):
        return halo_copy(i, 1, out.at[:, pl.ds(6, 3), pl.ds(48, 8)], cols.at[:, pl.ds(9, 3)], (lat, right))

    def halo_corner(i, out, cols):
        return halo_copy(i, 2, out.at[:, pl.ds(9, 3), pl.ds(48, 8)], cols.at[:, pl.ds(0, 3)], (up, right))

    def halo_rows(i, out, edge):
        return halo_copy(i, 3, out.at[:, pl.ds(9, 3), pl.ds(0, 48)], edge, (up, lon))

    def branch_of(wi):
        rows = pl.ds(pl.multiple_of(wi * TOK, TOK), TOK)
        o_s[rows, :] = mm3(split(mix[wi].T), wo)

    for i in range(10, 16):
        first_part[i] = jnp.zeros((16, 128), F32)
        second_part[i] = jnp.zeros((16, 128), F32)
    chunks[14, 0, 32:40, :] = jnp.zeros((8, 128), F32)
    chunks[14, 1] = jnp.zeros((40, 128), F32)
    chunks[15] = jnp.zeros((2, 40, 128), F32)

    head_of = lax.broadcasted_iota(jnp.int32, (TOK, D), 1) // HEAD

    @pl.loop(0, WINDOWS)
    def _(wi):
        @pl.when(wi == 3)
        def _():
            for copy in halos_in:
                copy.wait()
            front(3, WINDOWS)

        @pl.when(wi == 4)
        def _():
            table_gradient(0, first_part)
            first.start()
            pl.loop(0, 4)(branch_of)
            for w in range(4):
                scatter(w, o_s, out_b)
            halo_first(0, out_b, cols_b).start()

        @pl.when(wi == 7)
        def _():
            first.middle()

        rows = pl.ds(pl.multiple_of(wi * TOK, TOK), TOK)
        base = lax.div(wi, 4) * HEADS
        dv_acc = jnp.zeros((TOK, D), F32)
        dk_acc = jnp.zeros((TOK, D), F32)
        zero = jnp.zeros((TOK, D), BF16)
        for h in range(HEADS):
            blk = slice(h * 128, (h + 1) * 128)
            st = mm(kcat[rows, blk], qt[wi, h]) + bias[base + h]
            e = jnp.exp(st - jnp.max(st, axis=0, keepdims=True))
            p = e * (1.0 / jnp.sum(e, axis=0, keepdims=True))
            p_hi, p_lo = split(p)
            dp = mm(vcat[rows, blk], dot_[wi, h])
            ds = p * (dp - jnp.sum(p * dp, axis=0, keepdims=True))
            dsacc[base + h] += ds
            ds_hi, ds_lo = split(ds)
            v2 = vt[wi, h]
            m2 = mm(v2, p_hi)
            m = m2[:HEAD] + m2[HEAD:] + mm(v2[:HEAD], p_lo)
            mix_t[h * HEAD:(h + 1) * HEAD, :] = m
            k2 = kt[wi, h]
            g2 = mm(k2, ds_hi)
            g = g2[:HEAD] + g2[HEAD:] + mm(k2[:HEAD], ds_lo)
            dq[wi, h * HEAD:(h + 1) * HEAD, :] = g * factor
            mine = head_of == h
            o_hi = jnp.where(mine, do_hi[rows, :], zero)
            o_lo = jnp.where(mine, do_lo[rows, :], zero)
            dv_acc += mm(p_hi, o_hi) + mm(p_hi, o_lo) + mm(p_lo, o_hi)
            c_hi = jnp.where(mine, q_hi[rows, :], zero)
            c_lo = jnp.where(mine, q_lo[rows, :], zero)
            dk_acc += mm(ds_hi, c_hi) + mm(ds_hi, c_lo) + mm(ds_lo, c_hi)
        dv[rows, :] = dv_acc
        dk[rows, :] = dk_acc
        mix[wi] = mix_t[...]

    sums_ref[...] = jnp.zeros_like(sums_ref)

    @pl.loop(0, WINDOWS)
    def _(wi):
        rows = pl.ds(pl.multiple_of(wi * TOK, TOK), TOK)
        nt = split(xs[rows, :].T)
        sums_ref[:, 3 * D:] += mm3(split(mix[wi]), split(ups[rows, :]))
        sums_ref[:, :D] += mm3(nt, split(dq[wi].T))
        sums_ref[:, D:2 * D] += mm3(nt, split(dk[rows, :]))
        sums_ref[:, 2 * D:3 * D] += mm3(nt, split(dv[rows, :]))

    for i in range(24):
        for j in range(6):
            q, s = divmod(i * 6 + j, 5)
            chunks[q // 2, q % 2, s * 8:s * 8 + 8, :] = sums_ref[i * 8:i * 8 + 8, j * 128:(j + 1) * 128]
    pair = remote(chunks.at[:, 1 - core], recv_p, p_send, p_recv, (mate, lon))
    pair.start()
    table_gradient(1, second_part)
    pair.wait()
    half[...] = chunks[:, core] + recv_p[...]

    def plane_device(q):
        return (lax.div(q, 2) * 2 + core, z * 2 + lax.rem(q, 2))

    def stage_a(k):
        peer = lax.rem(plane + k, 16)
        return remote(half.at[peer], recv_a.at[k - 1], a_send.at[k - 1], a_recv.at[k - 1], plane_device(peer))

    @every(1, 16)
    def _(k):
        stage_a(k).start()

    second.start()

    pl.loop(4, WINDOWS)(branch_of)
    for wi in range(4, WINDOWS):
        scatter(wi, o_s, out_b)

    def own_copy(i, out, own):
        return pltpu.make_async_copy(out.at[:, pl.ds(0, 9), pl.ds(0, 48)], own, own_sem.at[i])

    own_copy(0, out_b, own_b).start()

    def rest_of(wi):
        rows = pl.ds(pl.multiple_of(wi * TOK, TOK), TOK)
        n = xs[rows, :]
        grad_scaled = (
            mm3(split(dq[wi].T), wqp, NT) + mm3(split(dk[rows, :]), wks, NT) + mm3(split(dv[rows, :]), wvs, NT)
        )
        g = grad_scaled * gain
        o_s[rows, :] = inv_s[rows, :][:, :1] * (
            g - jnp.mean(g, axis=-1, keepdims=True)
            - n * jnp.mean(g * n, axis=-1, keepdims=True)
        )

    pl.loop(4, WINDOWS)(rest_of)
    for wi in range(4, WINDOWS):
        scatter(wi, o_s, out_g)

    @every(1, 16)
    def _(k):
        stage_a(k).wait()

    own = half[plane]
    for k in range(15):
        own += recv_a[k]
    z_all[z] = own

    def stage_z(k, owner, peer):
        here = z_all.at[owner]
        return remote(here, here, z_send.at[k - 1], z_recv.at[k - 1], (lat, peer * 2 + y_hi))

    @every(1, 8)
    def _(k):
        stage_z(k, z, lax.rem(z + k, 8)).start()

    halo_second(0, out_b, cols_b).start()
    halo_corner(0, out_b, cols_b).start()
    halo_rows(0, out_b, rows_b).start()
    halo_rows(1, out_g, rows_g).start()
    second.middle()

    pl.loop(0, 4)(rest_of)
    for wi in range(4):
        scatter(wi, o_s, out_g)
    own_copy(1, out_g, own_g).start()

    @every(1, 8)
    def _(k):
        owner = lax.rem(z + 8 - k, 8)
        stage_z(k, owner, owner).wait_recv()

    whole = z_all[0]
    for k in range(1, 8):
        whole += z_all[k]
    total[plane, core] = whole

    def stage_d(k, owner, peer):
        here = total.at[owner, core]
        return remote(here, here, d_send.at[k - 1], d_recv.at[k - 1], plane_device(peer))

    @every(1, 16)
    def _(k):
        stage_d(k, plane, lax.rem(plane + k, 16)).start()

    halo_first(1, out_g, cols_g).start()
    halo_second(1, out_g, cols_g).start()
    halo_corner(1, out_g, cols_g).start()

    @every(1, 8)
    def _(k):
        stage_z(k, z, lax.rem(z + k, 8)).wait_send()

    @every(1, 16)
    def _(k):
        owner = lax.rem(plane + 16 - k, 16)
        stage_d(k, owner, owner).wait_recv()

    ours = total.at[:, core]
    swap = remote(ours, ours, m_send, m_recv, (mate, lon))
    swap.start()

    @every(1, 16)
    def _(k):
        stage_d(k, plane, lax.rem(plane + k, 16)).wait_send()

    first.end()
    second.end()
    own_copy(0, out_b, own_b).wait()
    own_copy(1, out_g, own_g).wait()
    for i, (out, edge, cols) in enumerate(((out_b, rows_b, cols_b), (out_g, rows_g, cols_g))):
        halo_rows(i, out, edge).wait()
        halo_first(i, out, cols).wait()
        halo_second(i, out, cols).wait()
        halo_corner(i, out, cols).wait()

    swap.wait_send()
    theirs = total.at[:, 1 - core]
    remote(theirs, theirs, m_send, m_recv, (mate, lon)).wait_recv()


def main(fields, cotangent, gain, wqkv, wout, table):
    vm = pl.BlockSpec(memory_space=pltpu.VMEM)
    anywhere = pl.BlockSpec(memory_space=pl.ANY)
    rows = WINDOWS * TOK
    DMA = pltpu.SemaphoreType.DMA
    scratch = [
        pltpu.VMEM((2, 12, 56, D), F32), pltpu.VMEM((2, 12, 56, D), F32),
        pltpu.VMEM((2, 12, 56, D), F32), pltpu.VMEM((2, 12, 56, D), F32),
        pltpu.VMEM((rows, D), F32), pltpu.VMEM((rows, D), F32), pltpu.VMEM((rows, 128), F32),
        pltpu.VMEM((rows, D), BF16), pltpu.VMEM((rows, D), BF16),
        pltpu.VMEM((rows, 768), BF16), pltpu.VMEM((rows, 768), BF16),
        pltpu.VMEM((rows, D), BF16), pltpu.VMEM((rows, D), BF16),
        pltpu.VMEM((rows, D), BF16), pltpu.VMEM((rows, D), BF16),
        pltpu.VMEM((WINDOWS, HEADS, 128, TOK), BF16),
        pltpu.VMEM((WINDOWS, HEADS, 64, TOK), BF16),
        pltpu.VMEM((WINDOWS, HEADS, 64, TOK), BF16),
        pltpu.VMEM((WINDOWS, HEADS, 128, TOK), BF16),
        pltpu.VMEM((2 * HEADS, TOK, TOK), F32),
        pltpu.VMEM((2 * HEADS, TOK, TOK), F32),
        pltpu.VMEM((TOK, WIN_LON, TOK), F32),
        pltpu.VMEM((WINDOWS, D, TOK), F32), pltpu.VMEM((WINDOWS, D, TOK), F32),
        pltpu.VMEM((rows, D), F32), pltpu.VMEM((rows, D), F32),
        pltpu.VMEM((D, TOK), F32),
        pltpu.VMEM((D, 4 * D), F32),
        pltpu.VMEM((16, 2, 40, 128), F32), pltpu.VMEM((16, 16, 128), F32), pltpu.VMEM((16, 16, 128), F32),
        pltpu.VMEM((16, 40, 128), F32), pltpu.VMEM((16, 40, 128), F32), pltpu.VMEM((15, 40, 128), F32),
        pltpu.VMEM((8, 40, 128), F32),
        pltpu.VMEM((15, 16, 128), F32), pltpu.VMEM((15, 16, 128), F32),
        pltpu.VMEM((TOK, OUTER * SPAN), F32), pltpu.VMEM((rows, D), F32),
        DMA((2,)), DMA((2,)), DMA((6,)), DMA((6,)), DMA((8,)), DMA((8,)), DMA, DMA, DMA((15,)), DMA((15,)),
        DMA((15,)), DMA((15,)), DMA((15,)), DMA((15,)), DMA((15,)), DMA((15,)),
        DMA((15,)), DMA((15,)), DMA, DMA, DMA((15,)), DMA((15,)), DMA((7,)), DMA((7,)),
    ]
    whole = jax.ShapeDtypeStruct((2, 9, 48, D), F32)
    edge = jax.ShapeDtypeStruct((2, 3, 48, D), F32)
    side = jax.ShapeDtypeStruct((2, 12, 8, D), F32)
    return pl.pallas_call(
        main_kernel,
        out_shape=[
            whole, whole, edge, edge, side, side,
            jax.ShapeDtypeStruct((16, 2, 40, 128), F32),
            jax.ShapeDtypeStruct((16, 16, 128), F32), jax.ShapeDtypeStruct((16, 16, 128), F32),
        ],
        in_specs=[anywhere] * 2 + [vm] * 4,
        out_specs=[anywhere] * 2 + [vm] * 7,
        scratch_shapes=scratch,
        compiler_params=pltpu.CompilerParams(
            collective_id=0, has_side_effects=True, vmem_limit_bytes=60 * 1024 * 1024),
    )(fields, cotangent, gain, wqkv, wout, table)


def finish_kernel(
    ext_b, ext_g, rows_b, rows_g, cols_b, cols_g, total, first_total, second_total, wqkv_ref, gain_ref,
    branch, grads, gain_out, qkv_out, out_out, table_out, full, flat,
):
    for ext, rows, cols, out in ((ext_b, rows_b, cols_b, branch), (ext_g, rows_g, cols_g, grads)):
        out[:, 0:3] = rows[...]
        out[:, 3:12] = ext[...]
        there = lax.broadcasted_iota(jnp.int32, (2, 12, 8, D), 2) < 6
        out[:, :, 0:8, :] = jnp.where(there, cols[...], out[:, :, 0:8, :])
    scale = 1.0 / math.sqrt(LATS * LONS * WINDOWS * TOK)
    for i in range(24):
        for j in range(6):
            q, s = divmod(i * 6 + j, 5)
            full[i * 8:i * 8 + 8, j * 128:(j + 1) * 128] = total[q // 2, q % 2, s * 8:s * 8 + 8, :] * scale
    raw = full[:, :3 * D]
    summed = jnp.sum(raw * wqkv_ref[...], axis=1, keepdims=True)
    gain_out[...] = jnp.broadcast_to(summed, (D, 128)).T[:1]
    qkv_out[...] = raw * jnp.broadcast_to(gain_ref[...], (8, D)).T[:, :1]
    out_out[...] = full[:, 3 * D:]
    def tile(ref, t):
        q, s = divmod(t, 2)
        return ref[q, s * 8:s * 8 + 8, :]

    for a, ref in enumerate((first_total, second_total)):
        for i in range(9):
            at = a * 72 + i * 8
            for j in range(2):
                flat[at:at + 8, j * 128:(j + 1) * 128] = tile(ref, i * 2 + j)
            packed = tile(ref, 18 + i // 6)
            turn = 20 * (i % 6)
            flat[at:at + 8, 256:384] = packed if turn == 0 else pltpu.roll(packed, 128 - turn, 1)
    for a in range(2):
        for h in range(HEADS):
            for i in range(OUTER):
                at = (a * HEADS + h) * OUTER + i
                table_out[h, a:a + 1, i * OUTER * SPAN:(i + 1) * OUTER * SPAN] = flat[at:at + 1, :OUTER * SPAN]


def finish(ext_b, ext_g, rows_b, rows_g, cols_b, cols_g, total, first_total, second_total, wqkv, gain):
    vm = pl.BlockSpec(memory_space=pltpu.VMEM)
    whole = jax.ShapeDtypeStruct((2, 12, 48, D), F32)
    return pl.pallas_call(
        finish_kernel,
        out_shape=[
            whole, whole, jax.ShapeDtypeStruct((1, D), F32), jax.ShapeDtypeStruct((D, 3 * D), F32),
            jax.ShapeDtypeStruct((D, D), F32), jax.ShapeDtypeStruct((HEADS, 2, OUTER * OUTER * SPAN), F32),
        ],
        in_specs=[vm] * 11,
        out_specs=[vm] * 6,
        scratch_shapes=[pltpu.VMEM((D, 4 * D), F32), pltpu.VMEM((TOK, 384), F32)],
        compiler_params=pltpu.CompilerParams(vmem_limit_bytes=60 * 1024 * 1024),
    )(ext_b, ext_g, rows_b, rows_g, cols_b, cols_g, total, first_total, second_total, wqkv, gain)


def on_device(fields, cotangent, norm_gain, qkv_weight, out_weight, bias_table):
    table = jnp.transpose(bias_table, (1, 0, 2))
    win_b, win_g, rows_b, rows_g, cols_b, cols_g, total, first_total, second_total = main(
        fields, cotangent, norm_gain.reshape(1, D), qkv_weight, out_weight, table)
    branch, grad_fields, gain, qkv, out, gtable = finish(
        win_b, win_g, rows_b, rows_g, cols_b, cols_g, total, first_total, second_total, qkv_weight, norm_gain.reshape(1, D))
    return branch, grad_fields, gain.reshape(D), qkv, out, jnp.transpose(gtable, (1, 0, 2))


def solution(mesh):
    cells = P(None, "lat", "lon", None)
    rows = P("lat", None, None)
    return jax.shard_map(
        on_device,
        mesh=mesh,
        in_specs=(cells, cells, P(), P(), P(), rows),
        out_specs=(cells, cells, P(), P(), P(), rows),
        check_vma=False,
    )
```

```python
import math
import jax
import jax.numpy as jnp
from jax import lax
from jax.experimental import pallas as pl
from jax.experimental.pallas import tpu as pltpu
from jax.sharding import PartitionSpec as P

WIN_LAT = 6
WIN_LON = 12
EPSILON = 1e-05
MASKED = -1000000000.0
HEADS = 6
HEAD = 32
D = 192
TOK = 144
WINDOWS = 8
OUTER = 12
SPAN = 23
F32 = jnp.float32
BF16 = jnp.bfloat16
NN = (((1,), (0,)), ((), ()))
NT = (((1,), (1,)), ((), ()))


def mm(a, b, dims=NN):
    return lax.dot_general(a, b, dims, preferred_element_type=F32)


def split(x):
    hi = x.astype(BF16)
    return hi, (x - hi.astype(F32)).astype(BF16)


def mm3(a, b, dims=NN):
    return mm(a[0], b[0], dims) + mm(a[0], b[1], dims) + mm(a[1], b[0], dims)


def selector(lo, length):
    row = lax.broadcasted_iota(jnp.int32, (length, TOK), 0)
    col = lax.broadcasted_iota(jnp.int32, (length, TOK), 1)
    picked = (col // WIN_LON) * SPAN + col % WIN_LON - lo + WIN_LON - 1
    return (row == picked).astype(F32).astype(BF16)


MESH = pl.DeviceIdType.MESH
LATS = 16
LONS = 16
CHIPS = 8


def remote(src, dst, send, recv, target):
    return pltpu.make_async_remote_copy(
        src_ref=src, dst_ref=dst, send_sem=send, recv_sem=recv, device_id=target, device_id_type=MESH)


def every(first, last):
    return pl.loop(first, last, unroll=True)


def main_kernel(
    f_ref, g_ref, gain_ref, wqkv_ref, wout_ref, table_ref,
    own_b, own_g, rows_b, rows_g, cols_b, cols_g, total, first_total, second_total,
    ext_f, ext_g, out_b, out_g,
    xs, ups, inv_s, s_hi, s_lo,
    kcat, vcat, q_hi, q_lo, do_hi, do_lo,
    qt, kt, vt, dot_, bias, dsacc, bias_raw,
    mix, dq, dk, dv, mix_t, sums_ref, chunks, first_part, second_part,
    half, recv_p, recv_a, z_all, first_recv, second_recv, tab_raw, o_s,
    local_sem, own_sem, in_send, in_recv, halo_send, halo_recv, p_send, p_recv, a_send, a_recv,
    t_send, t_recv, b_send, b_recv, c_send, c_recv, d_send, d_recv, m_send, m_recv, e_send, e_recv, z_send, z_recv,
):
    lat = lax.axis_index("lat")
    lon = lax.axis_index("lon")
    chip = lax.div(lat, 2)
    core = lax.rem(lat, 2)
    mate = chip * 2 + 1 - core
    y_hi = lax.rem(lon, 2)
    z = lax.div(lon, 2)
    plane = chip * 2 + y_hi
    up, down = lax.rem(lat + 1, LATS), lax.rem(lat + LATS - 1, LATS)
    right, left = lax.rem(lon + 1, LONS), lax.rem(lon + LONS - 1, LONS)
    local = []
    for i, (src, dst) in enumerate(((f_ref, ext_f), (g_ref, ext_g))):
        copy = pltpu.make_async_copy(
            src.at[:, pl.ds(3, 9)], dst.at[:, pl.ds(0, 9), pl.ds(0, 48)], local_sem.at[i])
        copy.start()
        local.append(copy)
    barrier = pltpu.get_barrier_semaphore()

    def greet(target):
        pl.semaphore_signal(barrier, inc=1, device_id=target, device_id_type=MESH)

    @every(1, LONS)
    def _(k):
        greet((lat, lax.rem(lon + k, LONS)))

    @every(1, CHIPS)
    def _(k):
        other = lax.rem(chip + k, CHIPS) * 2 + core
        greet((other, z * 2))
        greet((other, z * 2 + 1))

    greet((up, lon))
    greet((down, lon))
    greet((up, right))
    greet((down, left))

    factor = HEAD ** (-0.5)
    gain = gain_ref[...]
    w = wqkv_ref[...]
    wq = w[:, :D] * factor
    wk = w[:, D:2 * D]
    wv = w[:, 2 * D:]

    def replicated(m):
        parts = []
        for h in range(HEADS):
            parts += [m[:, h * HEAD:(h + 1) * HEAD]] * 4
        return jnp.concatenate(parts, axis=1)

    wkr = split(replicated(wk))
    wvr = split(replicated(wv))
    wqs = split(wq)
    wt = split(jnp.concatenate([wq.T, wk.T, wv.T], axis=0))
    wo = split(wout_ref[...])
    wks = split(wk)
    wvs = split(wv)
    wqp = split(w[:, :D])

    for a in range(2):
        for h in range(HEADS):
            for i in range(OUTER):
                at = (a * HEADS + h) * OUTER + i
                tab_raw[at:at + 1, :] = table_ref[h, a:a + 1, i * OUTER * SPAN:(i + 1) * OUTER * SPAN]
    t0 = tab_raw[...]
    t_hi = t0.astype(BF16)
    rest = t0 - t_hi.astype(F32)
    t_mid = rest.astype(BF16)
    t_lo = (rest - t_mid.astype(F32)).astype(BF16)
    for lo in range(WIN_LON):
        sel = selector(lo, OUTER * SPAN)
        bias_raw[:, lo, :] = mm(t_hi, sel) + mm(t_mid, sel) + mm(t_lo, sel)
    row = lax.broadcasted_iota(jnp.int32, (TOK, TOK), 0)
    col = lax.broadcasted_iota(jnp.int32, (TOK, TOK), 1)
    half_r = (row // WIN_LON) % WIN_LAT < WIN_LAT // 2
    half_c = (col // WIN_LON) % WIN_LAT < WIN_LAT // 2
    apart = half_r != half_c
    for a in range(2):
        on_seam = lat * 2 + a == 31
        cut = jnp.logical_and(apart, on_seam)
        for h in range(HEADS):
            g = a * HEADS + h
            b = bias_raw[g * OUTER:(g + 1) * OUTER].reshape(TOK, TOK)
            bias[g] = jnp.where(cut, MASKED, b.T)
            dsacc[g] = jnp.zeros((TOK, TOK), F32)

    def front(first_window, last_window):
        for wi in range(first_window, last_window):
            a, b = divmod(wi, 4)
            for l in range(2):
                for r in range(WIN_LAT):
                    at = wi * TOK + (l * WIN_LAT + r) * WIN_LON
                    c0 = 6 + WIN_LON * b
                    xs[at:at + WIN_LON, :] = ext_f[l, a * WIN_LAT + r, c0:c0 + WIN_LON, :]
                    ups[at:at + WIN_LON, :] = ext_g[l, a * WIN_LAT + r, c0:c0 + WIN_LON, :]

        @pl.loop(first_window, last_window)
        def _(wi):
            rows = pl.ds(pl.multiple_of(wi * TOK, TOK), TOK)
            x = xs[rows, :]
            c = x - jnp.mean(x, axis=-1, keepdims=True)
            inv = lax.rsqrt(jnp.mean(c * c, axis=-1, keepdims=True) + EPSILON)
            n = c * inv
            xs[rows, :] = n
            inv_s[rows, :] = jnp.broadcast_to(inv, (TOK, 128))
            s = split(n * gain)
            s_hi[rows, :] = s[0]
            s_lo[rows, :] = s[1]
            pt = mm3(wt, s, NT)
            for i, ref in enumerate((qt, kt, vt)):
                ph, pll = split(pt[i * D:(i + 1) * D])
                for h in range(HEADS):
                    a_, b_ = ph[h * HEAD:(h + 1) * HEAD], pll[h * HEAD:(h + 1) * HEAD]
                    if ref is qt:
                        ref[wi, h] = jnp.concatenate([a_, b_, a_, b_], axis=0)
                    else:
                        ref[wi, h] = jnp.concatenate([a_, b_], axis=0)
            u = split(ups[rows, :])
            dt = split(mm3(wo, u, NT))
            for h in range(HEADS):
                a_, b_ = dt[0][h * HEAD:(h + 1) * HEAD], dt[1][h * HEAD:(h + 1) * HEAD]
                dot_[wi, h] = jnp.concatenate([a_, b_, a_, b_], axis=0)

        size = (last_window - first_window) * TOK
        rows = slice(first_window * TOK, last_window * TOK)
        first_half = lax.broadcasted_iota(jnp.int32, (size, 256), 1) % 128 < 64
        left_side = (s_hi[rows, :], s_lo[rows, :])
        for j in range(3):
            cols = slice(j * 256, (j + 1) * 256)
            for wr, ref in ((wkr, kcat), (wvr, vcat)):
                ph, pll = split(mm3(left_side, (wr[0][:, cols], wr[1][:, cols])))
                ref[rows, cols] = jnp.where(first_half, ph, pll)
        qh, ql = split(mm3(left_side, wqs))
        q_hi[rows, :] = qh
        q_lo[rows, :] = ql
        dh, dl = split(mm3(split(ups[rows, :]), wo, NT))
        do_hi[rows, :] = dh
        do_lo[rows, :] = dl

    pl.semaphore_wait(barrier, 33)
    halos_in = []
    for i, (src, dst) in enumerate(((f_ref, ext_f), (g_ref, ext_g))):
        pieces = (
            (src.at[:, pl.ds(3, 9), pl.ds(0, 8)], dst.at[:, pl.ds(0, 9), pl.ds(48, 8)], (lat, left)),
            (src.at[:, pl.ds(0, 3), pl.ds(0, 8)], dst.at[:, pl.ds(9, 3), pl.ds(48, 8)], (down, left)),
            (src.at[:, pl.ds(0, 3)], dst.at[:, pl.ds(9, 3), pl.ds(0, 48)], (down, lon)),
        )
        for j, (a, b, target) in enumerate(pieces):
            copy = remote(a, b, in_send.at[i * 3 + j], in_recv.at[i * 3 + j], target)
            copy.start()
            halos_in.append(copy)

    for copy in local:
        copy.wait()
    front(0, 3)
    class LonSum:
        def __init__(self, src, recv, out, s1, r1, s2, r2):
            self.refs = src, recv, out, s1, r1, s2, r2

        def scatter_copy(self, k):
            src, recv, out, s1, r1, s2, r2 = self.refs
            peer = lax.rem(lon + k, LONS)
            return remote(src.at[peer], recv.at[k - 1], s1.at[k - 1], r1.at[k - 1], (lat, peer))

        def gather_copy(self, k, owner, peer):
            src, recv, out, s1, r1, s2, r2 = self.refs
            return remote(out.at[owner], out.at[owner], s2.at[k - 1], r2.at[k - 1], (lat, peer))

        def start(self):
            @every(1, LONS)
            def _(k):
                self.scatter_copy(k).start()

        def middle(self):
            src, recv, out = self.refs[:3]

            @every(1, LONS)
            def _(k):
                self.scatter_copy(k).wait()

            own = src[lon]
            for k in range(LONS - 1):
                own += recv[k]
            out[lon] = own

            @every(1, LONS)
            def _(k):
                self.gather_copy(k, lon, lax.rem(lon + k, LONS)).start()

        def end(self):
            @every(1, LONS)
            def _(k):
                self.gather_copy(k, lon, lax.rem(lon + k, LONS)).wait_send()
                owner = lax.rem(lon + LONS - k, LONS)
                self.gather_copy(k, owner, owner).wait_recv()

    first = LonSum(first_part, first_recv, first_total, t_send, t_recv, e_send, e_recv)
    second = LonSum(second_part, second_recv, second_total, b_send, b_recv, c_send, c_recv)

    def place(ref, t, value):
        q, s = divmod(t, 2)
        ref[q, s * 8:s * 8 + 8, :] = value

    def table_gradient(a, ref):
        for g in range(a * HEADS, (a + 1) * HEADS):
            bias_raw[g * OUTER:(g + 1) * OUTER] = dsacc[g].T.reshape(OUTER, WIN_LON, TOK)
        acc = jnp.zeros((72, 384), F32)
        for lo in range(WIN_LON):
            sel = selector(lo, 384)
            d_hi, d_lo = split(bias_raw[a * 72:(a + 1) * 72, lo, :])
            acc += mm(d_hi, sel, NT) + mm(d_lo, sel, NT)
        for i in range(9):
            for j in range(2):
                place(ref, i * 2 + j, acc[i * 8:i * 8 + 8, j * 128:(j + 1) * 128])
        for p, members in enumerate((range(6), range(6, 9))):
            packed = jnp.zeros((8, 128), F32)
            for i in members:
                tail = acc[i * 8:i * 8 + 8, 256:]
                turn = 20 * (i % 6)
                packed += tail if turn == 0 else pltpu.roll(tail, turn, 1)
            place(ref, 18 + p, packed)

    def scatter(wi, src, out):
        a, b = divmod(wi, 4)
        for l in range(2):
            for r in range(WIN_LAT):
                at = wi * TOK + (l * WIN_LAT + r) * WIN_LON
                c0 = 6 + WIN_LON * b
                out[l, a * WIN_LAT + r, c0:c0 + WIN_LON, :] = src[at:at + WIN_LON, :]

    def halo_copy(i, j, src, dst, target):
        return remote(src, dst, halo_send.at[i * 4 + j], halo_recv.at[i * 4 + j], target)

    def halo_first(i, out, cols):
        return halo_copy(i, 0, out.at[:, pl.ds(0, 6), pl.ds(48, 8)], cols.at[:, pl.ds(3, 6)], (lat, right))

    def halo_second(i, out, cols):
        return halo_copy(i, 1, out.at[:, pl.ds(6, 3), pl.ds(48, 8)], cols.at[:, pl.ds(9, 3)], (lat, right))

    def halo_corner(i, out, cols):
        return halo_copy(i, 2, out.at[:, pl.ds(9, 3), pl.ds(48, 8)], cols.at[:, pl.ds(0, 3)], (up, right))

    def halo_rows(i, out, edge):
        return halo_copy(i, 3, out.at[:, pl.ds(9, 3), pl.ds(0, 48)], edge, (up, lon))

    def branch_of(wi):
        rows = pl.ds(pl.multiple_of(wi * TOK, TOK), TOK)
        o_s[rows, :] = mm3(split(mix[wi].T), wo)

    for i in range(10, 16):
        first_part[i] = jnp.zeros((16, 128), F32)
        second_part[i] = jnp.zeros((16, 128), F32)
    chunks[14, 0, 32:40, :] = jnp.zeros((8, 128), F32)
    chunks[14, 1] = jnp.zeros((40, 128), F32)
    chunks[15] = jnp.zeros((2, 40, 128), F32)

    head_of = lax.broadcasted_iota(jnp.int32, (TOK, D), 1) // HEAD

    @pl.loop(0, WINDOWS)
    def _(wi):
        @pl.when(wi == 3)
        def _():
            for copy in halos_in:
                copy.wait()
            front(3, WINDOWS)

        @pl.when(wi == 4)
        def _():
            table_gradient(0, first_part)
            first.start()
            pl.loop(0, 4)(branch_of)
            for w in range(4):
                scatter(w, o_s, out_b)
            halo_first(0, out_b, cols_b).start()

        @pl.when(wi == 7)
        def _():
            first.middle()

        rows = pl.ds(pl.multiple_of(wi * TOK, TOK), TOK)
        base = lax.div(wi, 4) * HEADS
        dv_acc = jnp.zeros((TOK, D), F32)
        dk_acc = jnp.zeros((TOK, D), F32)
        zero = jnp.zeros((TOK, D), BF16)
        for h in range(HEADS):
            blk = slice(h * 128, (h + 1) * 128)
            st = mm(kcat[rows, blk], qt[wi, h]) + bias[base + h]
            e = jnp.exp(st - jnp.max(st, axis=0, keepdims=True))
            p = e * (1.0 / jnp.sum(e, axis=0, keepdims=True))
            p_hi, p_lo = split(p)
            dp = mm(vcat[rows, blk], dot_[wi, h])
            ds = p * (dp - jnp.sum(p * dp, axis=0, keepdims=True))
            dsacc[base + h] += ds
            ds_hi, ds_lo = split(ds)
            v2 = vt[wi, h]
            m2 = mm(v2, p_hi)
            m = m2[:HEAD] + m2[HEAD:] + mm(v2[:HEAD], p_lo)
            mix_t[h * HEAD:(h + 1) * HEAD, :] = m
            k2 = kt[wi, h]
            g2 = mm(k2, ds_hi)
            g = g2[:HEAD] + g2[HEAD:] + mm(k2[:HEAD], ds_lo)
            dq[wi, h * HEAD:(h + 1) * HEAD, :] = g * factor
            mine = head_of == h
            o_hi = jnp.where(mine, do_hi[rows, :], zero)
            o_lo = jnp.where(mine, do_lo[rows, :], zero)
            dv_acc += mm(p_hi, o_hi) + mm(p_hi, o_lo) + mm(p_lo, o_hi)
            c_hi = jnp.where(mine, q_hi[rows, :], zero)
            c_lo = jnp.where(mine, q_lo[rows, :], zero)
            dk_acc += mm(ds_hi, c_hi) + mm(ds_hi, c_lo) + mm(ds_lo, c_hi)
        dv[rows, :] = dv_acc
        dk[rows, :] = dk_acc
        mix[wi] = mix_t[...]

    sums_ref[...] = jnp.zeros_like(sums_ref)

    @pl.loop(0, WINDOWS)
    def _(wi):
        rows = pl.ds(pl.multiple_of(wi * TOK, TOK), TOK)
        nt = split(xs[rows, :].T)
        sums_ref[:, 3 * D:] += mm3(split(mix[wi]), split(ups[rows, :]))
        sums_ref[:, :D] += mm3(nt, split(dq[wi].T))
        sums_ref[:, D:2 * D] += mm3(nt, split(dk[rows, :]))
        sums_ref[:, 2 * D:3 * D] += mm3(nt, split(dv[rows, :]))

    for i in range(24):
        for j in range(6):
            q, s = divmod(i * 6 + j, 5)
            chunks[q // 2, q % 2, s * 8:s * 8 + 8, :] = sums_ref[i * 8:i * 8 + 8, j * 128:(j + 1) * 128]
    pair = remote(chunks.at[:, 1 - core], recv_p, p_send, p_recv, (mate, lon))
    pair.start()
    table_gradient(1, second_part)
    pair.wait()
    half[...] = chunks[:, core] + recv_p[...]

    def plane_device(q):
        return (lax.div(q, 2) * 2 + core, z * 2 + lax.rem(q, 2))

    def stage_a(k):
        peer = lax.rem(plane + k, 16)
        return remote(half.at[peer], recv_a.at[k - 1], a_send.at[k - 1], a_recv.at[k - 1], plane_device(peer))

    @every(1, 16)
    def _(k):
        stage_a(k).start()

    second.start()

    pl.loop(4, WINDOWS)(branch_of)
    for wi in range(4, WINDOWS):
        scatter(wi, o_s, out_b)

    def own_copy(i, out, own):
        return pltpu.make_async_copy(out.at[:, pl.ds(0, 9), pl.ds(0, 48)], own, own_sem.at[i])

    own_copy(0, out_b, own_b).start()

    def rest_of(wi):
        rows = pl.ds(pl.multiple_of(wi * TOK, TOK), TOK)
        n = xs[rows, :]
        grad_scaled = (
            mm3(split(dq[wi].T), wqp, NT) + mm3(split(dk[rows, :]), wks, NT) + mm3(split(dv[rows, :]), wvs, NT)
        )
        g = grad_scaled * gain
        o_s[rows, :] = inv_s[rows, :][:, :1] * (
            g - jnp.mean(g, axis=-1, keepdims=True)
            - n * jnp.mean(g * n, axis=-1, keepdims=True)
        )

    pl.loop(4, WINDOWS)(rest_of)
    for wi in range(4, WINDOWS):
        scatter(wi, o_s, out_g)

    @every(1, 16)
    def _(k):
        stage_a(k).wait()

    own = half[plane]
    for k in range(15):
        own += recv_a[k]
    z_all[z] = own

    def stage_z(k, owner, peer):
        here = z_all.at[owner]
        return remote(here, here, z_send.at[k - 1], z_recv.at[k - 1], (lat, peer * 2 + y_hi))

    @every(1, 8)
    def _(k):
        stage_z(k, z, lax.rem(z + k, 8)).start()

    halo_second(0, out_b, cols_b).start()
    halo_corner(0, out_b, cols_b).start()
    halo_rows(0, out_b, rows_b).start()
    halo_rows(1, out_g, rows_g).start()
    second.middle()

    pl.loop(0, 4)(rest_of)
    for wi in range(4):
        scatter(wi, o_s, out_g)
    own_copy(1, out_g, own_g).start()

    @every(1, 8)
    def _(k):
        owner = lax.rem(z + 8 - k, 8)
        stage_z(k, owner, owner).wait_recv()

    whole = z_all[0]
    for k in range(1, 8):
        whole += z_all[k]
    total[plane, core] = whole

    def stage_d(k, owner, peer):
        here = total.at[owner, core]
        return remote(here, here, d_send.at[k - 1], d_recv.at[k - 1], plane_device(peer))

    @every(1, 16)
    def _(k):
        stage_d(k, plane, lax.rem(plane + k, 16)).start()

    halo_first(1, out_g, cols_g).start()
    halo_second(1, out_g, cols_g).start()
    halo_corner(1, out_g, cols_g).start()

    @every(1, 8)
    def _(k):
        stage_z(k, z, lax.rem(z + k, 8)).wait_send()

    @every(1, 16)
    def _(k):
        owner = lax.rem(plane + 16 - k, 16)
        stage_d(k, owner, owner).wait_recv()

    ours = total.at[:, core]
    swap = remote(ours, ours, m_send, m_recv, (mate, lon))
    swap.start()

    @every(1, 16)
    def _(k):
        stage_d(k, plane, lax.rem(plane + k, 16)).wait_send()

    first.end()
    second.end()
    own_copy(0, out_b, own_b).wait()
    own_copy(1, out_g, own_g).wait()
    for i, (out, edge, cols) in enumerate(((out_b, rows_b, cols_b), (out_g, rows_g, cols_g))):
        halo_rows(i, out, edge).wait()
        halo_first(i, out, cols).wait()
        halo_second(i, out, cols).wait()
        halo_corner(i, out, cols).wait()

    swap.wait_send()
    theirs = total.at[:, 1 - core]
    remote(theirs, theirs, m_send, m_recv, (mate, lon)).wait_recv()


def main(fields, cotangent, gain, wqkv, wout, table):
    vm = pl.BlockSpec(memory_space=pltpu.VMEM)
    anywhere = pl.BlockSpec(memory_space=pl.ANY)
    rows = WINDOWS * TOK
    DMA = pltpu.SemaphoreType.DMA
    scratch = [
        pltpu.VMEM((2, 12, 56, D), F32), pltpu.VMEM((2, 12, 56, D), F32),
        pltpu.VMEM((2, 12, 56, D), F32), pltpu.VMEM((2, 12, 56, D), F32),
        pltpu.VMEM((rows, D), F32), pltpu.VMEM((rows, D), F32), pltpu.VMEM((rows, 128), F32),
        pltpu.VMEM((rows, D), BF16), pltpu.VMEM((rows, D), BF16),
        pltpu.VMEM((rows, 768), BF16), pltpu.VMEM((rows, 768), BF16),
        pltpu.VMEM((rows, D), BF16), pltpu.VMEM((rows, D), BF16),
        pltpu.VMEM((rows, D), BF16), pltpu.VMEM((rows, D), BF16),
        pltpu.VMEM((WINDOWS, HEADS, 128, TOK), BF16),
        pltpu.VMEM((WINDOWS, HEADS, 64, TOK), BF16),
        pltpu.VMEM((WINDOWS, HEADS, 64, TOK), BF16),
        pltpu.VMEM((WINDOWS, HEADS, 128, TOK), BF16),
        pltpu.VMEM((2 * HEADS, TOK, TOK), F32),
        pltpu.VMEM((2 * HEADS, TOK, TOK), F32),
        pltpu.VMEM((TOK, WIN_LON, TOK), F32),
        pltpu.VMEM((WINDOWS, D, TOK), F32), pltpu.VMEM((WINDOWS, D, TOK), F32),
        pltpu.VMEM((rows, D), F32), pltpu.VMEM((rows, D), F32),
        pltpu.VMEM((D, TOK), F32),
        pltpu.VMEM((D, 4 * D), F32),
        pltpu.VMEM((16, 2, 40, 128), F32), pltpu.VMEM((16, 16, 128), F32), pltpu.VMEM((16, 16, 128), F32),
        pltpu.VMEM((16, 40, 128), F32), pltpu.VMEM((16, 40, 128), F32), pltpu.VMEM((15, 40, 128), F32),
        pltpu.VMEM((8, 40, 128), F32),
        pltpu.VMEM((15, 16, 128), F32), pltpu.VMEM((15, 16, 128), F32),
        pltpu.VMEM((TOK, OUTER * SPAN), F32), pltpu.VMEM((rows, D), F32),
        DMA((2,)), DMA((2,)), DMA((6,)), DMA((6,)), DMA((8,)), DMA((8,)), DMA, DMA, DMA((15,)), DMA((15,)),
        DMA((15,)), DMA((15,)), DMA((15,)), DMA((15,)), DMA((15,)), DMA((15,)),
        DMA((15,)), DMA((15,)), DMA, DMA, DMA((15,)), DMA((15,)), DMA((7,)), DMA((7,)),
    ]
    whole = jax.ShapeDtypeStruct((2, 9, 48, D), F32)
    edge = jax.ShapeDtypeStruct((2, 3, 48, D), F32)
    side = jax.ShapeDtypeStruct((2, 12, 8, D), F32)
    return pl.pallas_call(
        main_kernel,
        out_shape=[
            whole, whole, edge, edge, side, side,
            jax.ShapeDtypeStruct((16, 2, 40, 128), F32),
            jax.ShapeDtypeStruct((16, 16, 128), F32), jax.ShapeDtypeStruct((16, 16, 128), F32),
        ],
        in_specs=[anywhere] * 2 + [vm] * 4,
        out_specs=[anywhere] * 2 + [vm] * 7,
        scratch_shapes=scratch,
        compiler_params=pltpu.CompilerParams(
            collective_id=0, has_side_effects=True, vmem_limit_bytes=60 * 1024 * 1024),
    )(fields, cotangent, gain, wqkv, wout, table)


def finish_kernel(
    ext_b, ext_g, rows_b, rows_g, cols_b, cols_g, total, first_total, second_total, wqkv_ref, gain_ref,
    branch, grads, gain_out, qkv_out, out_out, table_out, full, flat,
):
    for ext, rows, cols, out in ((ext_b, rows_b, cols_b, branch), (ext_g, rows_g, cols_g, grads)):
        out[:, 0:3] = rows[...]
        out[:, 3:12] = ext[...]
        there = lax.broadcasted_iota(jnp.int32, (2, 12, 8, D), 2) < 6
        out[:, :, 0:8, :] = jnp.where(there, cols[...], out[:, :, 0:8, :])
    scale = 1.0 / math.sqrt(LATS * LONS * WINDOWS * TOK)
    for i in range(24):
        for j in range(6):
            q, s = divmod(i * 6 + j, 5)
            full[i * 8:i * 8 + 8, j * 128:(j + 1) * 128] = total[q // 2, q % 2, s * 8:s * 8 + 8, :] * scale
    raw = full[:, :3 * D]
    summed = jnp.sum(raw * wqkv_ref[...], axis=1, keepdims=True)
    gain_out[...] = jnp.broadcast_to(summed, (D, 128)).T[:1]
    qkv_out[...] = raw * jnp.broadcast_to(gain_ref[...], (8, D)).T[:, :1]
    out_out[...] = full[:, 3 * D:]
    def tile(ref, t):
        q, s = divmod(t, 2)
        return ref[q, s * 8:s * 8 + 8, :]

    for a, ref in enumerate((first_total, second_total)):
        for i in range(9):
            at = a * 72 + i * 8
            for j in range(2):
                flat[at:at + 8, j * 128:(j + 1) * 128] = tile(ref, i * 2 + j)
            packed = tile(ref, 18 + i // 6)
            turn = 20 * (i % 6)
            flat[at:at + 8, 256:384] = packed if turn == 0 else pltpu.roll(packed, 128 - turn, 1)
    for a in range(2):
        for h in range(HEADS):
            for i in range(OUTER):
                at = (a * HEADS + h) * OUTER + i
                table_out[h, a:a + 1, i * OUTER * SPAN:(i + 1) * OUTER * SPAN] = flat[at:at + 1, :OUTER * SPAN]


def finish(ext_b, ext_g, rows_b, rows_g, cols_b, cols_g, total, first_total, second_total, wqkv, gain):
    vm = pl.BlockSpec(memory_space=pltpu.VMEM)
    whole = jax.ShapeDtypeStruct((2, 12, 48, D), F32)
    return pl.pallas_call(
        finish_kernel,
        out_shape=[
            whole, whole, jax.ShapeDtypeStruct((1, D), F32), jax.ShapeDtypeStruct((D, 3 * D), F32),
            jax.ShapeDtypeStruct((D, D), F32), jax.ShapeDtypeStruct((HEADS, 2, OUTER * OUTER * SPAN), F32),
        ],
        in_specs=[vm] * 11,
        out_specs=[vm] * 6,
        scratch_shapes=[pltpu.VMEM((D, 4 * D), F32), pltpu.VMEM((TOK, 384), F32)],
        compiler_params=pltpu.CompilerParams(vmem_limit_bytes=60 * 1024 * 1024),
    )(ext_b, ext_g, rows_b, rows_g, cols_b, cols_g, total, first_total, second_total, wqkv, gain)


def on_device(fields, cotangent, norm_gain, qkv_weight, out_weight, bias_table):
    table = jnp.transpose(bias_table, (1, 0, 2))
    win_b, win_g, rows_b, rows_g, cols_b, cols_g, total, first_total, second_total = main(
        fields, cotangent, norm_gain.reshape(1, D), qkv_weight, out_weight, table)
    branch, grad_fields, gain, qkv, out, gtable = finish(
        win_b, win_g, rows_b, rows_g, cols_b, cols_g, total, first_total, second_total, qkv_weight, norm_gain.reshape(1, D))
    return branch, grad_fields, gain.reshape(D), qkv, out, jnp.transpose(gtable, (1, 0, 2))


def solution(mesh):
    cells = P(None, "lat", "lon", None)
    rows = P("lat", None, None)
    return jax.shard_map(
        on_device,
        mesh=mesh,
        in_specs=(cells, cells, P(), P(), P(), rows),
        out_specs=(cells, cells, P(), P(), P(), rows),
        check_vma=False,
    )
```
